32 devices in a mesh: dp: 2 (over x), seq: 16 (over z, y, core).
Axes of the slice: x: 2, y: 2, z: 4, core: 2. Of those that a mesh axis runs over, the one named last changes fastest.
Arguments:
- queries: bfloat16 [2, 2048, 4096], P('dp', 'seq'), may hold values from -5 to 5
- rotated_key_rows: bfloat16 [2, 2048, 512], P('dp', 'seq'), may hold values from -5 to 5
- hidden_states: bfloat16 [2, 2048, 8192], P('dp', 'seq'), may hold values from -6 to 6
- block_order: int32 [32], replicated, may hold values from 0 to 31, each once
- first_weight: bfloat16 [8192, 512], replicated, may hold values from -0.0625 to 0.0625
- first_bias: float32 [512], replicated, may hold values from -3 to 3
- output_weight: bfloat16 [4, 512], replicated, may hold values from -0.25 to 0.25
- output_bias: float32 [4], replicated, may hold values from -1 to 1
Outputs:
- token_attention_mass: float32 [2, 4, 2048], P('dp', None, 'seq')
- loss_value: float32 [], replicated
- step_first: float32 [8192, 512], P('seq')
- output_weight_step: float32 [4, 512], replicated
- step_bias: float32 [512], replicated
- grad_bias: float32 [4], replicated
The draws below stay inside these ranges and needn't reach their ends.
All inputs are finite; a program needn't handle non-finite values.
Results may differ from the reference program's by a relative error of at most 0.0023.
Values may be sent and summed in bfloat16 or wider, within the bound.
No kernel may reach another device: no remote copies, remote signals or barrier semaphores. Data moves between devices by JAX's collectives and lax.ppermute only.
A program may use at most 64 MiB of HBM per device.

```python
import math
import jax
import jax.numpy as jnp
from jax import lax

D = 8192
HQ = 32
KEY_VALUE_HEADS = 4
HEAD_SIZE = 128
RETAIN_HIDDEN = 512
BLK = 64
QUERY_GROUP_SIZE = 8
SEQUENCE_LENGTH = 2048
BLOCKS = 32
SEQUENCE_COUNT = 2


def draw_queries(key, part):
    value_rows = jnp.clip(0.3 * jax.random.normal(jax.random.fold_in(key, 31), (SEQUENCE_COUNT, SEQUENCE_LENGTH, KEY_VALUE_HEADS, QUERY_GROUP_SIZE, HEAD_SIZE)), -5.0, 5.0)
    return value_rows.reshape(SEQUENCE_COUNT, SEQUENCE_LENGTH, HQ * HEAD_SIZE).astype(jnp.bfloat16)


def draw_rotated_key_rows(key, part):
    value_rows = jnp.clip(0.3 * jax.random.normal(jax.random.fold_in(key, 32), (SEQUENCE_COUNT, SEQUENCE_LENGTH, KEY_VALUE_HEADS, HEAD_SIZE)), -5.0, 5.0)
    return value_rows.reshape(SEQUENCE_COUNT, SEQUENCE_LENGTH, KEY_VALUE_HEADS * HEAD_SIZE).astype(jnp.bfloat16)


def block_scale(stream_key, extent, cuts, least, high):
    level, own = 1.0, jax.random.fold_in(stream_key, 6)
    for axis_at, blocks in cuts:
        heights = jnp.exp(jax.random.uniform(jax.random.fold_in(own, axis_at), (blocks,), jnp.float32, least / len(cuts), high / len(cuts)))
        level = level * jnp.repeat(heights, extent[axis_at] // blocks).reshape([-1 if axis == axis_at else 1 for axis in range(len(extent))])
    return level


def noise(key, shape, width, reach, pieces=(), held_as=jnp.bfloat16):
    gain = block_scale(key, shape, pieces, -0.22, 0.18) if pieces else 1.0
    drawn = jax.random.normal(key, shape, jnp.float32) * width * gain
    return jnp.minimum(jnp.maximum(drawn, -reach), reach).astype(held_as)


def setup_inputs(seed: int = 0) -> dict:
    key_list = jax.random.split(jax.random.key(seed), 9)
    queries = draw_queries(jax.random.fold_in(key_list[8], 71), 0)
    rotated_key_rows = draw_rotated_key_rows(jax.random.fold_in(key_list[8], 71), 0)
    hidden_states = noise(key_list[2], (SEQUENCE_COUNT, SEQUENCE_LENGTH, D), 1.0, 6.0, ((0, 2), (1, 16)))
    block_order = jax.random.permutation(key_list[3], BLOCKS).astype(jnp.int32)
    first_weight = noise(key_list[4], (D, RETAIN_HIDDEN), D ** -0.5, 0.0625)
    first_bias = noise(key_list[5], (RETAIN_HIDDEN,), 0.5, 3.0, (), jnp.float32)
    output_weight = noise(key_list[6], (KEY_VALUE_HEADS, RETAIN_HIDDEN), RETAIN_HIDDEN ** -0.5, 0.25)
    output_bias = jnp.clip(jax.random.uniform(key_list[7], (KEY_VALUE_HEADS,), jnp.float32, -1.0, 1.0), -1.0, 1.0)
    return {"queries": queries, "rotated_key_rows": rotated_key_rows, "hidden_states": hidden_states, "block_order": block_order, "first_weight": first_weight, "first_bias": first_bias, "output_weight": output_weight, "output_bias": output_bias}


def places(block_order):
    row_ids = jnp.arange(SEQUENCE_LENGTH, dtype=jnp.int32)
    return block_order[row_ids // BLK].astype(jnp.int32) * BLK + row_ids % BLK

def sequence_mass(queries, rotated_key_rows, places_all):
    head_queries = queries.astype(jnp.float32).reshape(SEQUENCE_LENGTH, KEY_VALUE_HEADS, QUERY_GROUP_SIZE, HEAD_SIZE)
    head_keys = rotated_key_rows.astype(jnp.float32).reshape(SEQUENCE_LENGTH, KEY_VALUE_HEADS, HEAD_SIZE)
    height = math.gcd(SEQUENCE_LENGTH, 128)

    def visit_block(carried, step_index):
        query_block = lax.dynamic_slice_in_dim(head_queries, step_index * height, height, 0)
        query_pos = lax.dynamic_slice_in_dim(places_all, step_index * height, height, 0)
        scores = jnp.einsum('tkgd,nkd->kgtn', query_block, head_keys, precision=lax.Precision.HIGHEST) * HEAD_SIZE ** (-0.5)
        visible = query_pos[:, None] >= places_all[None, :]
        masked = jnp.where(visible, scores, -1e+30)
        highest = lax.optimization_barrier(jnp.max(masked, axis=-1))
        summed = lax.optimization_barrier(jnp.sum(jnp.where(visible, jnp.exp(masked - highest[..., None]), 0.0), axis=-1))
        log_total = highest + jnp.log(summed)
        weights = jnp.where(visible, jnp.exp(masked - log_total[..., None]), 0.0)
        return (carried + lax.optimization_barrier(jnp.sum(weights, axis=(1, 2))) / QUERY_GROUP_SIZE, None)
    every_step = jnp.arange(SEQUENCE_LENGTH // height, dtype=jnp.int32)
    key_attention_mass, ignored_value = lax.scan(visit_block, jnp.zeros((KEY_VALUE_HEADS, SEQUENCE_LENGTH), jnp.float32), every_step)
    return key_attention_mass

def normalized_scores(value_rows):
    return value_rows / jnp.sqrt(jnp.mean(value_rows * value_rows) + 1e-06)

def reference(queries, rotated_key_rows, hidden_states, block_order, first_weight, first_bias, output_weight, output_bias):
    places_all = places(block_order)
    token_attention_mass = lax.map(lambda paired: sequence_mass(paired[0], paired[1], places_all), (queries, rotated_key_rows))
    tokens_in = hidden_states.reshape(SEQUENCE_COUNT * SEQUENCE_LENGTH, D)
    pre_act = jnp.dot(tokens_in, first_weight, preferred_element_type=jnp.float32) + first_bias
    hidden = jax.nn.silu(pre_act).astype(jnp.bfloat16)
    predicted_scores = lax.dot_general(output_weight, hidden, (((1,), (1,)), ((), ())), preferred_element_type=jnp.float32) + output_bias[:, None]
    target_rows = jnp.transpose(token_attention_mass, (1, 0, 2)).reshape(KEY_VALUE_HEADS, SEQUENCE_COUNT * SEQUENCE_LENGTH)
    score_residue = predicted_scores - jnp.log(1.0 + target_rows)
    loss_value = 0.5 * jnp.sum(score_residue * score_residue) / SEQUENCE_LENGTH
    out_grad = score_residue / SEQUENCE_LENGTH
    grad_bias = lax.optimization_barrier(jnp.sum(out_grad, axis=1))
    grad_second = jnp.dot(out_grad, hidden.astype(jnp.float32), precision=lax.Precision.HIGHEST)
    back_grad = jnp.dot(out_grad.T, output_weight.astype(jnp.float32), precision=lax.Precision.HIGHEST)
    gate_value = jax.nn.sigmoid(pre_act)
    slope_grad = back_grad * gate_value * (1.0 + pre_act * (1.0 - gate_value))
    grad_first_bias = lax.optimization_barrier(jnp.sum(slope_grad, axis=0))
    slope_half = slope_grad.astype(jnp.bfloat16)
    grad_first = lax.dot_general(tokens_in, slope_half, (((0,), (0,)), ((), ())), preferred_element_type=jnp.float32)
    return (token_attention_mass, loss_value, normalized_scores(grad_first), normalized_scores(grad_second), normalized_scores(grad_first_bias), grad_bias)
```

```python
import functools

import jax
import jax.numpy as jnp
from jax import lax
from jax.experimental import pallas as pl
from jax.experimental.pallas import tpu as pltpu
from jax.sharding import PartitionSpec as P

KEY_VALUE_HEADS = 4
HEAD_SIZE = 128
BLK = 64
QUERY_GROUP_SIZE = 8
LOG2_E = 1.4426950408889634
VMEM_LIMIT = 60 * 1024 * 1024
VMEM = pl.BlockSpec(memory_space=pltpu.VMEM)
SMEM = pl.BlockSpec(memory_space=pltpu.SMEM)


def swap(value, axis, mask):
    return lax.ppermute(value, axis, [(i, i ^ mask) for i in range(lax.axis_size(axis))])


def gather_xor(value, axis):
    amount = lax.axis_size(axis)
    top = amount // 4
    slots = {0: value}
    for step in (1, 2, 3):
        slots[step * top] = swap(value, axis, step * top)
    for mask in range(2, top, 2):
        for step in range(4):
            slots[step * top + mask] = swap(slots[step * top], axis, mask)
    for mask in range(0, amount, 2):
        slots[mask + 1] = swap(slots[mask], axis, 1)
    return [slots[k] for k in range(amount)]


def split3(value):
    high = value.astype(jnp.bfloat16)
    rest = value - high.astype(jnp.float32)
    middle = rest.astype(jnp.bfloat16)
    low = (rest - middle.astype(jnp.float32)).astype(jnp.bfloat16)
    return high, middle, low


def attention_kernel(slots, place_ref, order_ref, query_ref, *refs):
    key_refs, mass_ref = refs[:slots], refs[slots]
    keys, bias, scores, mixed = refs[slots + 1 :]
    rows = key_refs[0].shape[0]
    total = rows * slots
    pairs = query_ref.shape[0]
    lanes = query_ref.shape[1]
    per_head = pairs // KEY_VALUE_HEADS
    chunk = 256
    blocks = rows // BLK
    me = place_ref[0]
    scale = HEAD_SIZE ** (-0.5) * LOG2_E

    def pos_of(owner, index):
        at = jnp.zeros(index.shape, jnp.int32)
        for b in range(blocks):
            at = jnp.where(index // BLK == b, order_ref[owner * blocks + b], at)
        return at * BLK + index % BLK

    query_pos = pos_of(me, lax.broadcasted_iota(jnp.int32, (rows, rows), 1))
    key_index = lax.broadcasted_iota(jnp.int32, (rows, rows), 0)
    for k in range(slots):
        at = pl.ds(k * rows, rows)
        for head in range(KEY_VALUE_HEADS):
            keys[head, at, :] = key_refs[k][:, head * HEAD_SIZE : (head + 1) * HEAD_SIZE]
        bias[at, :] = jnp.where(pos_of(me ^ k, key_index) <= query_pos, 0.0, -1e30)

    def visit_head(head, carried):
        mixed[...] = jnp.zeros_like(mixed)

        def visit_pair(pair, also):
            query = query_ref[head * per_head + pair]
            top = jnp.full((8, lanes), -1e30, jnp.float32)
            for c in range(total // chunk):
                at = pl.ds(c * chunk, chunk)
                raw = lax.dot_general(
                    keys[head, at, :],
                    query,
                    (((1,), (1,)), ((), ())),
                    preferred_element_type=jnp.float32,
                )
                shade = bias[at, :]
                raw = raw + jnp.concatenate([shade] * (lanes // rows), axis=1)
                scores[at, :] = raw
                top = jnp.maximum(top, jnp.max(raw.reshape(chunk // 8, 8, lanes), axis=0))
            top = jnp.max(top, axis=0, keepdims=True)
            summed = jnp.zeros((8, lanes), jnp.float32)
            for c in range(total // chunk):
                at = pl.ds(c * chunk, chunk)
                weight = jnp.exp2((scores[at, :] - top) * scale)
                scores[at, :] = weight
                summed = summed + jnp.sum(weight.reshape(chunk // 8, 8, lanes), axis=0)
            share = (1.0 / QUERY_GROUP_SIZE) / jnp.sum(summed, axis=0, keepdims=True)
            for c in range(total // chunk):
                at = pl.ds(c * chunk, chunk)
                part = scores[at, :] * share
                gathered = mixed[at, :]
                for j in range(lanes // rows):
                    gathered = gathered + part[:, j * rows : (j + 1) * rows]
                mixed[at, :] = gathered
            return also

        lax.fori_loop(0, per_head, visit_pair, 0)
        for k in range(slots):
            tile = jnp.transpose(mixed[pl.ds(k * rows, rows), :])
            mass_ref[me ^ k, pl.ds(head, 1), :] = jnp.sum(tile, axis=0, keepdims=True)
        return carried

    lax.fori_loop(0, KEY_VALUE_HEADS, visit_head, 0)


def attention_mass(place, block_order, queries, key_slots):
    slots = len(key_slots)
    rows = queries.shape[0]
    heads = queries.shape[1] // HEAD_SIZE
    total = rows * slots
    fold = 2
    arranged = jnp.transpose(queries.reshape(rows, heads, HEAD_SIZE), (1, 0, 2))
    arranged = arranged.reshape(heads // fold, fold * rows, HEAD_SIZE)
    return pl.pallas_call(
        functools.partial(attention_kernel, slots),
        out_shape=jax.ShapeDtypeStruct((slots, KEY_VALUE_HEADS, rows), jnp.float32),
        in_specs=[SMEM, SMEM, VMEM] + [VMEM] * slots,
        out_specs=VMEM,
        scratch_shapes=[
            pltpu.VMEM((KEY_VALUE_HEADS, total, HEAD_SIZE), jnp.bfloat16),
            pltpu.VMEM((total, rows), jnp.float32),
            pltpu.VMEM((total, fold * rows), jnp.float32),
            pltpu.VMEM((total, rows), jnp.float32),
        ],
        compiler_params=pltpu.CompilerParams(vmem_limit_bytes=VMEM_LIMIT),
        cost_estimate=pl.CostEstimate(
            flops=2 * rows * total * heads * HEAD_SIZE,
            bytes_accessed=2 * rows * heads * HEAD_SIZE,
            transcendentals=rows * total * heads,
        ),
    )(place, block_order, arranged, *key_slots)


def gradient_kernel(slots, dp, place_ref, message_ref, columns_ref, output_ref, hidden_ref, *refs):
    slope_refs = refs[:slots]
    grad_ref, mass_ref, small_ref = refs[slots : slots + 3]
    out_grad, slope, wide, grad = refs[slots + 3 :]
    me, part = place_ref[0], place_ref[1]
    rows = hidden_ref.shape[0]
    total = rows * slots
    units = hidden_ref.shape[1]
    mass = jnp.sum(message_ref[:, :slots], axis=0)
    out_grad[...] = mass
    mass_ref[...] = out_grad[me]
    residue = message_ref[:, slots] - jnp.log(1.0 + mass)
    out_grad[...] = residue / total
    loss_sum = jnp.sum(residue * residue) * (0.5 / total)
    grad_bias = jnp.sum(jnp.sum(out_grad[...], axis=0), axis=1, keepdims=True)
    output_rows = output_ref[...]
    output_three = jnp.concatenate([output_rows] * 3, axis=0)
    first_bias = jnp.zeros((8, units), jnp.float32)
    for k in range(slots):
        owner = me ^ k
        scaled = out_grad[owner] * message_ref[owner, slots + 1]
        back = lax.dot_general(
            jnp.concatenate(split3(scaled), axis=0),
            output_three,
            (((0,), (0,)), ((), ())),
            preferred_element_type=jnp.float32,
        )
        fall = back * slope_refs[k][...].astype(jnp.float32)
        first_bias = first_bias + jnp.sum(fall.reshape(rows // 8, 8, units), axis=0)
        slope[pl.ds(pl.multiple_of(owner * rows, rows), rows), :] = fall.astype(jnp.bfloat16)
        wide[:, k * rows : (k + 1) * rows] = columns_ref[k]
    grad[...] = jnp.dot(wide[...], slope[...], preferred_element_type=jnp.float32)
    share = grad.shape[0] // dp
    for k in range(dp):
        grad_ref[k] = grad[pl.ds(pl.multiple_of((part ^ k) * share, share), share), :]
    second = lax.dot_general(
        jnp.concatenate(split3(out_grad[me]), axis=0),
        hidden_ref[...],
        (((1,), (0,)), ((), ())),
        preferred_element_type=jnp.float32,
    )
    heads = KEY_VALUE_HEADS
    second = second[:heads] + second[heads : 2 * heads] + second[2 * heads :]
    small_ref[pl.ds(0, heads), :] = second
    small_ref[pl.ds(heads, 1), :] = jnp.sum(first_bias, axis=0, keepdims=True)
    small_ref[pl.ds(heads + 1, 1), :] = jnp.full((1, units), loss_sum, jnp.float32)
    small_ref[pl.ds(heads + 2, heads), :] = jnp.broadcast_to(grad_bias, (heads, units))
    small_ref[pl.ds(2 * heads + 2, 6), :] = jnp.zeros((6, units), jnp.float32)


def gradient(place, message, columns, output_weight, hidden, slope_slots, dp):
    slots = len(slope_slots)
    rows, units = hidden.shape
    depth = columns.shape[1]
    return pl.pallas_call(
        functools.partial(gradient_kernel, slots, dp),
        out_shape=(
            jax.ShapeDtypeStruct((dp, depth // dp, units), jnp.float32),
            jax.ShapeDtypeStruct((KEY_VALUE_HEADS, rows), jnp.float32),
            jax.ShapeDtypeStruct((16, units), jnp.float32),
        ),
        in_specs=[SMEM] + [VMEM] * (4 + slots),
        out_specs=(VMEM, VMEM, VMEM),
        scratch_shapes=[
            pltpu.VMEM((slots, KEY_VALUE_HEADS, rows), jnp.float32),
            pltpu.VMEM((slots * rows, units), jnp.bfloat16),
            pltpu.VMEM((depth, slots * rows), jnp.bfloat16),
            pltpu.VMEM((depth, units), jnp.float32),
        ],
        compiler_params=pltpu.CompilerParams(vmem_limit_bytes=VMEM_LIMIT),
    )(place, message, columns, output_weight, hidden, *slope_slots)


def square_kernel(parts, small_ref, *refs):
    part_refs, total_ref, send_ref = refs[:parts], refs[parts], refs[parts + 1]
    total = part_refs[0][...]
    for part_ref in part_refs[1:]:
        total = total + part_ref[...]
    total_ref[...] = total
    units = total.shape[1]
    square = jnp.sum(jnp.sum(total * total, axis=0, keepdims=True), axis=1, keepdims=True)
    row = KEY_VALUE_HEADS * 2 + 2
    send_ref[...] = small_ref[...]
    send_ref[pl.ds(row, 1), :] = jnp.broadcast_to(square, (1, units))


def squares(small, parts):
    return pl.pallas_call(
        functools.partial(square_kernel, len(parts)),
        out_shape=(
            jax.ShapeDtypeStruct(parts[0].shape, jnp.float32),
            jax.ShapeDtypeStruct(small.shape, jnp.float32),
        ),
        in_specs=[VMEM] * (1 + len(parts)),
        out_specs=(VMEM, VMEM),
        compiler_params=pltpu.CompilerParams(vmem_limit_bytes=VMEM_LIMIT),
    )(small, *parts)


def scale_kernel(slots, dp, entries, place_ref, message_ref, *refs):
    part_refs = refs[:dp]
    step_ref, second_ref, first_bias_ref, bias_ref, loss_ref = refs[dp:]
    part = place_ref[1]
    heads = KEY_VALUE_HEADS
    total = jnp.sum(message_ref[...], axis=0)
    once = message_ref[0]
    for d in range(1, dp):
        once = once + message_ref[d * slots]
    square = total[2 * heads + 2 : 2 * heads + 3, :1]
    inverse = 1.0 / jnp.sqrt(square / entries + 1e-06)
    share = part_refs[0].shape[0]
    for k in range(dp):
        at = pl.ds(pl.multiple_of((part ^ k) * share, share), share)
        step_ref[at, :] = part_refs[k][...] * inverse
    second = total[:heads]
    spread = jnp.sum(jnp.sum(second * second, axis=0, keepdims=True), axis=1, keepdims=True)
    second_ref[...] = second / jnp.sqrt(spread / second.size + 1e-06)
    first_bias = once[heads : heads + 1]
    spread = jnp.sum(first_bias * first_bias, axis=1, keepdims=True)
    first_bias_ref[...] = first_bias / jnp.sqrt(spread / first_bias.size + 1e-06)
    loss_ref[...] = once[heads + 1 : heads + 2, :128]
    bias_ref[...] = once[heads + 2 : 2 * heads + 2, :128]


def scaled(place, message, parts, slots, entries):
    dp = len(parts)
    share, units = parts[0].shape
    return pl.pallas_call(
        functools.partial(scale_kernel, slots, dp, entries),
        out_shape=(
            jax.ShapeDtypeStruct((dp * share, units), jnp.float32),
            jax.ShapeDtypeStruct((KEY_VALUE_HEADS, units), jnp.float32),
            jax.ShapeDtypeStruct((1, units), jnp.float32),
            jax.ShapeDtypeStruct((KEY_VALUE_HEADS, 128), jnp.float32),
            jax.ShapeDtypeStruct((1, 128), jnp.float32),
        ),
        in_specs=[SMEM] + [VMEM] * (1 + dp),
        out_specs=(VMEM,) * 5,
        compiler_params=pltpu.CompilerParams(vmem_limit_bytes=VMEM_LIMIT),
    )(place, message, *parts)


def send_all(value, axes, amount):
    copies = jnp.broadcast_to(value[None], (amount,) + value.shape)
    return lax.all_to_all(copies, axes, 0, 0, tiled=True)


def per_device(
    queries,
    rotated_key_rows,
    hidden_states,
    block_order,
    first_weight,
    first_bias,
    output_weight,
    output_bias,
):
    seq, dp = lax.axis_size("seq"), lax.axis_size("dp")
    rows, model = hidden_states.shape[1:]
    units = first_weight.shape[1]
    place = jnp.stack([lax.axis_index("seq"), lax.axis_index("dp")]).astype(jnp.int32)
    tokens = hidden_states.reshape(rows, model)

    key_slots = gather_xor(rotated_key_rows.reshape(rows, -1), "seq")
    columns = lax.all_to_all(
        jnp.transpose(tokens).reshape(seq, model // seq, rows), "seq", 0, 0, tiled=True
    )

    pre_act = jnp.dot(tokens, first_weight, preferred_element_type=jnp.float32) + first_bias
    gate = jax.nn.sigmoid(pre_act)
    hidden = (pre_act * gate).astype(jnp.bfloat16)
    predicted = (
        lax.dot_general(
            output_weight, hidden, (((1,), (1,)), ((), ())), preferred_element_type=jnp.float32
        )
        + output_bias[:, None]
    )
    fall = gate * (1.0 + pre_act * (1.0 - gate))
    reach = jnp.maximum(jnp.max(jnp.abs(fall), axis=1), 1e-30)
    fall_slots = gather_xor((fall / reach[:, None]).astype(jnp.float16), "seq")

    mass = attention_mass(place, block_order, queries.reshape(rows, -1), key_slots)
    reach_rows = jnp.broadcast_to(reach[None, None, :], (1,) + predicted.shape)
    message = jnp.concatenate([mass, predicted[None], reach_rows], axis=0)
    message = send_all(message, "seq", seq)

    slope_slots = [fall_slot.astype(jnp.float32) for fall_slot in fall_slots]
    grads, own_mass, small = gradient(
        place, message, columns, output_weight, hidden, slope_slots, dp
    )
    parts = [grads[0]] + [swap(grads[k], "dp", k) for k in range(1, dp)]
    total, small = squares(small, parts)
    totals = [total] + [swap(total, "dp", k) for k in range(1, dp)]
    message = send_all(small, ("dp", "seq"), dp * seq)
    step_first, second, bias_step, bias, loss = scaled(
        place, message, totals, seq, model * units
    )
    return (
        own_mass.reshape(1, KEY_VALUE_HEADS, rows),
        loss[0, 0],
        step_first,
        second,
        bias_step.reshape(units),
        bias[:, 0],
    )


def solution(mesh):
    tokens = P("dp", "seq", None)
    return jax.shard_map(
        per_device,
        mesh=mesh,
        in_specs=(tokens, tokens, tokens, P(), P(), P(), P(), P()),
        out_specs=(P("dp", None, "seq"), P(), P("seq", None), P(), P(), P()),
        check_vma=False,
    )
```

```python
import functools

import jax
import jax.numpy as jnp
from jax import lax
from jax.experimental import pallas as pl
from jax.experimental.pallas import tpu as pltpu
from jax.sharding import PartitionSpec as P

KEY_VALUE_HEADS = 4
HEAD_SIZE = 128
BLK = 64
QUERY_GROUP_SIZE = 8
LOG2_E = 1.4426950408889634
VMEM_LIMIT = 60 * 1024 * 1024
VMEM = pl.BlockSpec(memory_space=pltpu.VMEM)
SMEM = pl.BlockSpec(memory_space=pltpu.SMEM)


def swap(value, axis, mask):
    return lax.ppermute(value, axis, [(i, i ^ mask) for i in range(lax.axis_size(axis))])


def gather_far(value, axis):
    top = lax.axis_size(axis) // 4
    return [value] + [swap(value, axis, step * top) for step in (1, 2, 3)]


def gather_even(far, axis):
    top = lax.axis_size(axis) // 4
    slots = {step * top: far[step] for step in range(4)}
    for mask in range(2, top, 2):
        for step in range(4):
            slots[step * top + mask] = swap(slots[step * top], axis, mask)
    return [slots[k] for k in range(0, 4 * top, 2)]


def gather_xor(far, axis):
    pairs = [(slot, swap(slot, axis, 1)) for slot in gather_even(far, axis)]
    return [slot for pair in pairs for slot in pair]


def split3(value):
    high = value.astype(jnp.bfloat16)
    rest = value - high.astype(jnp.float32)
    middle = rest.astype(jnp.bfloat16)
    low = (rest - middle.astype(jnp.float32)).astype(jnp.bfloat16)
    return high, middle, low


def attention_kernel(slots, place_ref, order_ref, query_ref, *refs):
    key_refs, predicted_ref, reach_ref, mass_ref = refs[:slots], *refs[slots : slots + 3]
    keys, bias, scores, mixed = refs[slots + 3 :]
    rows = key_refs[0].shape[0]
    total = rows * slots
    pairs = query_ref.shape[0]
    lanes = query_ref.shape[1]
    per_head = pairs // KEY_VALUE_HEADS
    chunk = 256
    blocks = rows // BLK
    me = place_ref[0]
    scale = HEAD_SIZE ** (-0.5) * LOG2_E

    def pos_of(owner, index):
        at = jnp.zeros(index.shape, jnp.int32)
        for b in range(blocks):
            at = jnp.where(index // BLK == b, order_ref[owner * blocks + b], at)
        return at * BLK + index % BLK

    mass_ref[...] = jnp.zeros_like(mass_ref)
    mass_ref[me, KEY_VALUE_HEADS:, :] = predicted_ref[...]
    beside = mass_ref.shape[0] - slots
    spot = lax.broadcasted_iota(jnp.int32, (beside, 8, rows), 0) * 8
    spot = spot + lax.broadcasted_iota(jnp.int32, (beside, 8, rows), 1)
    mass_ref[slots:] = jnp.where(spot == me, reach_ref[...][None], 0.0)
    query_pos = pos_of(me, lax.broadcasted_iota(jnp.int32, (rows, rows), 1))
    key_index = lax.broadcasted_iota(jnp.int32, (rows, rows), 0)
    for k in range(slots):
        at = pl.ds(k * rows, rows)
        for head in range(KEY_VALUE_HEADS):
            keys[head, at, :] = key_refs[k][:, head * HEAD_SIZE : (head + 1) * HEAD_SIZE]
        bias[at, :] = jnp.where(pos_of(me ^ k, key_index) <= query_pos, 0.0, -1e30)

    def visit_head(head, carried):
        mixed[...] = jnp.zeros_like(mixed)

        def visit_pair(pair, also):
            query = query_ref[head * per_head + pair]
            top = jnp.full((8, lanes), -1e30, jnp.float32)
            for c in range(total // chunk):
                at = pl.ds(c * chunk, chunk)
                raw = lax.dot_general(
                    keys[head, at, :],
                    query,
                    (((1,), (1,)), ((), ())),
                    preferred_element_type=jnp.float32,
                )
                shade = bias[at, :]
                raw = raw + jnp.concatenate([shade] * (lanes // rows), axis=1)
                scores[at, :] = raw
                top = jnp.maximum(top, jnp.max(raw.reshape(chunk // 8, 8, lanes), axis=0))
            top = jnp.max(top, axis=0, keepdims=True)
            summed = jnp.zeros((8, lanes), jnp.float32)
            for c in range(total // chunk):
                at = pl.ds(c * chunk, chunk)
                weight = jnp.exp2((scores[at, :] - top) * scale)
                scores[at, :] = weight
                summed = summed + jnp.sum(weight.reshape(chunk // 8, 8, lanes), axis=0)
            share = (1.0 / QUERY_GROUP_SIZE) / jnp.sum(summed, axis=0, keepdims=True)
            for c in range(total // chunk):
                at = pl.ds(c * chunk, chunk)
                part = scores[at, :] * share
                gathered = mixed[at, :]
                for j in range(lanes // rows):
                    gathered = gathered + part[:, j * rows : (j + 1) * rows]
                mixed[at, :] = gathered
            return also

        lax.fori_loop(0, per_head, visit_pair, 0)
        for k in range(slots):
            tile = jnp.transpose(mixed[pl.ds(k * rows, rows), :])
            mass_ref[me ^ k, pl.ds(head, 1), :] = jnp.sum(tile, axis=0, keepdims=True)
        return carried

    lax.fori_loop(0, KEY_VALUE_HEADS, visit_head, 0)


def attention_mass(place, block_order, queries, key_slots, predicted, reach):
    slots = len(key_slots)
    rows = queries.shape[0]
    heads = queries.shape[1] // HEAD_SIZE
    total = rows * slots
    fold = 2
    arranged = jnp.transpose(queries.reshape(rows, heads, HEAD_SIZE), (1, 0, 2))
    arranged = arranged.reshape(heads // fold, fold * rows, HEAD_SIZE)
    return pl.pallas_call(
        functools.partial(attention_kernel, slots),
        out_shape=jax.ShapeDtypeStruct((slots + slots // 8, 8, rows), jnp.float32),
        in_specs=[SMEM, SMEM, VMEM] + [VMEM] * (slots + 2),
        out_specs=VMEM,
        scratch_shapes=[
            pltpu.VMEM((KEY_VALUE_HEADS, total, HEAD_SIZE), jnp.bfloat16),
            pltpu.VMEM((total, rows), jnp.float32),
            pltpu.VMEM((total, fold * rows), jnp.float32),
            pltpu.VMEM((total, rows), jnp.float32),
        ],
        compiler_params=pltpu.CompilerParams(vmem_limit_bytes=VMEM_LIMIT),
        cost_estimate=pl.CostEstimate(
            flops=2 * rows * total * heads * HEAD_SIZE,
            bytes_accessed=2 * rows * heads * HEAD_SIZE,
            transcendentals=rows * total * heads,
        ),
    )(place, block_order, arranged, *key_slots, predicted, reach)


def gradient_kernel(slots, dp, place_ref, columns_ref, output_ref, hidden_ref, *refs):
    message_refs, fall_refs = refs[:4], refs[4:6]
    grad_ref, mass_ref, small_ref = refs[6:9]
    out_grad, slope, wide, grad, reaches = refs[9:]
    me, part = place_ref[0], place_ref[1]
    rows = hidden_ref.shape[0]
    total = rows * slots
    units = hidden_ref.shape[1]
    message = (message_refs[0][...] + message_refs[1][...]) + (
        message_refs[2][...] + message_refs[3][...]
    )
    for k in range(slots):
        reaches[k] = message[slots + k // 8, k % 8 : k % 8 + 1, :]
    mass = message[:slots, :KEY_VALUE_HEADS]
    out_grad[...] = mass
    mass_ref[...] = out_grad[me]
    residue = message[:slots, KEY_VALUE_HEADS:] - jnp.log(1.0 + mass)
    out_grad[...] = residue / total
    loss_sum = jnp.sum(residue * residue) * (0.5 / total)
    grad_bias = jnp.sum(jnp.sum(out_grad[...], axis=0), axis=1, keepdims=True)
    output_rows = output_ref[...]
    output_three = jnp.concatenate([output_rows] * 3, axis=0)
    first_bias = jnp.zeros((8, units), jnp.float32)
    for k in range(slots):
        owner = me ^ k
        scaled = out_grad[owner] * reaches[owner]
        back = lax.dot_general(
            jnp.concatenate(split3(scaled), axis=0),
            output_three,
            (((0,), (0,)), ((), ())),
            preferred_element_type=jnp.float32,
        )
        fall = back * fall_refs[k % 2][k // 2]
        first_bias = first_bias + jnp.sum(fall.reshape(rows // 8, 8, units), axis=0)
        slope[pl.ds(pl.multiple_of(owner * rows, rows), rows), :] = fall.astype(jnp.bfloat16)
        wide[:, k * rows : (k + 1) * rows] = columns_ref[k]
    grad[...] = jnp.dot(wide[...], slope[...], preferred_element_type=jnp.float32)
    share = grad.shape[0] // dp
    for k in range(dp):
        grad_ref[k] = grad[pl.ds(pl.multiple_of((part ^ k) * share, share), share), :]
    second = lax.dot_general(
        jnp.concatenate(split3(out_grad[me]), axis=0),
        hidden_ref[...],
        (((1,), (0,)), ((), ())),
        preferred_element_type=jnp.float32,
    )
    heads = KEY_VALUE_HEADS
    second = second[:heads] + second[heads : 2 * heads] + second[2 * heads :]
    small_ref[pl.ds(0, heads), :] = second
    small_ref[pl.ds(heads, 1), :] = jnp.sum(first_bias, axis=0, keepdims=True)
    small_ref[pl.ds(heads + 1, 1), :] = jnp.full((1, units), loss_sum, jnp.float32)
    small_ref[pl.ds(heads + 2, heads), :] = jnp.broadcast_to(grad_bias, (heads, units))
    small_ref[pl.ds(2 * heads + 2, 6), :] = jnp.zeros((6, units), jnp.float32)


def gradient(place, messages, columns, output_weight, hidden, falls, dp):
    slots = 2 * falls[0].shape[0]
    rows, units = hidden.shape
    depth = columns.shape[1]
    return pl.pallas_call(
        functools.partial(gradient_kernel, slots, dp),
        out_shape=(
            jax.ShapeDtypeStruct((dp, depth // dp, units), jnp.float32),
            jax.ShapeDtypeStruct((KEY_VALUE_HEADS, rows), jnp.float32),
            jax.ShapeDtypeStruct((16, units), jnp.float32),
        ),
        in_specs=[SMEM] + [VMEM] * 9,
        out_specs=(VMEM, VMEM, VMEM),
        scratch_shapes=[
            pltpu.VMEM((slots, KEY_VALUE_HEADS, rows), jnp.float32),
            pltpu.VMEM((slots * rows, units), jnp.bfloat16),
            pltpu.VMEM((depth, slots * rows), jnp.bfloat16),
            pltpu.VMEM((depth, units), jnp.float32),
            pltpu.VMEM((slots, 1, rows), jnp.float32),
        ],
        compiler_params=pltpu.CompilerParams(vmem_limit_bytes=VMEM_LIMIT),
    )(place, columns, output_weight, hidden, *messages, *falls)


def square_kernel(parts, small_ref, *refs):
    part_refs, total_ref, send_ref = refs[:parts], refs[parts], refs[parts + 1]
    total = part_refs[0][...]
    for part_ref in part_refs[1:]:
        total = total + part_ref[...]
    total_ref[...] = total
    units = total.shape[1]
    square = jnp.sum(jnp.sum(total * total, axis=0, keepdims=True), axis=1, keepdims=True)
    row = KEY_VALUE_HEADS * 2 + 2
    send_ref[...] = small_ref[...]
    send_ref[pl.ds(row, 1), :] = jnp.broadcast_to(square, (1, units))


def squares(small, parts):
    return pl.pallas_call(
        functools.partial(square_kernel, len(parts)),
        out_shape=(
            jax.ShapeDtypeStruct(parts[0].shape, jnp.float32),
            jax.ShapeDtypeStruct(small.shape, jnp.float32),
        ),
        in_specs=[VMEM] * (1 + len(parts)),
        out_specs=(VMEM, VMEM),
        compiler_params=pltpu.CompilerParams(vmem_limit_bytes=VMEM_LIMIT),
    )(small, *parts)


def scale_kernel(slots, dp, entries, place_ref, message_ref, *refs):
    part_refs = refs[:dp]
    step_ref, second_ref, first_bias_ref, bias_ref, loss_ref = refs[dp:]
    part = place_ref[1]
    heads = KEY_VALUE_HEADS
    total = jnp.sum(message_ref[...], axis=0)
    once = message_ref[0]
    for d in range(1, dp):
        once = once + message_ref[d * slots]
    square = total[2 * heads + 2 : 2 * heads + 3, :1]
    inverse = 1.0 / jnp.sqrt(square / entries + 1e-06)
    share = part_refs[0].shape[0]
    for k in range(dp):
        at = pl.ds(pl.multiple_of((part ^ k) * share, share), share)
        step_ref[at, :] = part_refs[k][...] * inverse
    second = total[:heads]
    spread = jnp.sum(jnp.sum(second * second, axis=0, keepdims=True), axis=1, keepdims=True)
    second_ref[...] = second / jnp.sqrt(spread / second.size + 1e-06)
    first_bias = once[heads : heads + 1]
    spread = jnp.sum(first_bias * first_bias, axis=1, keepdims=True)
    first_bias_ref[...] = first_bias / jnp.sqrt(spread / first_bias.size + 1e-06)
    loss_ref[...] = once[heads + 1 : heads + 2, :128]
    bias_ref[...] = once[heads + 2 : 2 * heads + 2, :128]


def scaled(place, message, parts, slots, entries):
    dp = len(parts)
    share, units = parts[0].shape
    return pl.pallas_call(
        functools.partial(scale_kernel, slots, dp, entries),
        out_shape=(
            jax.ShapeDtypeStruct((dp * share, units), jnp.float32),
            jax.ShapeDtypeStruct((KEY_VALUE_HEADS, units), jnp.float32),
            jax.ShapeDtypeStruct((1, units), jnp.float32),
            jax.ShapeDtypeStruct((KEY_VALUE_HEADS, 128), jnp.float32),
            jax.ShapeDtypeStruct((1, 128), jnp.float32),
        ),
        in_specs=[SMEM] + [VMEM] * (1 + dp),
        out_specs=(VMEM,) * 5,
        compiler_params=pltpu.CompilerParams(vmem_limit_bytes=VMEM_LIMIT),
    )(place, message, *parts)


def send_all(value, axes, amount):
    copies = jnp.broadcast_to(value[None], (amount,) + value.shape)
    return lax.all_to_all(copies, axes, 0, 0, tiled=True)


def per_device(
    queries,
    rotated_key_rows,
    hidden_states,
    block_order,
    first_weight,
    first_bias,
    output_weight,
    output_bias,
):
    seq, dp = lax.axis_size("seq"), lax.axis_size("dp")
    rows, model = hidden_states.shape[1:]
    units = first_weight.shape[1]
    place = jnp.stack([lax.axis_index("seq"), lax.axis_index("dp")]).astype(jnp.int32)
    tokens = hidden_states.reshape(rows, model)

    key_slots = gather_xor(gather_far(rotated_key_rows.reshape(rows, -1), "seq"), "seq")
    columns = lax.all_to_all(
        jnp.transpose(tokens).reshape(seq, model // seq, rows), "seq", 0, 0, tiled=True
    )

    pre_act = jnp.dot(tokens, first_weight, preferred_element_type=jnp.float32) + first_bias
    gate = jax.nn.sigmoid(pre_act)
    hidden = (pre_act * gate).astype(jnp.bfloat16)
    predicted = (
        lax.dot_general(
            output_weight, hidden, (((1,), (1,)), ((), ())), preferred_element_type=jnp.float32
        )
        + output_bias[:, None]
    )
    fall = gate * (1.0 + pre_act * (1.0 - gate))
    reach = jnp.maximum(jnp.max(jnp.abs(fall), axis=1), 1e-30)
    fall_far = gather_far((fall / reach[:, None]).astype(jnp.float16), "seq")

    message = attention_mass(
        place, block_order, queries.reshape(rows, -1), key_slots, predicted, reach[None]
    )
    message, *fall_far = lax.optimization_barrier((message, *fall_far))
    falls = jnp.stack(gather_even(fall_far, "seq"))
    falls = [falls.astype(jnp.float32), swap(falls, "seq", 1).astype(jnp.float32)]
    mask = 1
    while mask < seq // 4:
        message = message + swap(message, "seq", mask)
        mask *= 2
    messages = gather_far(message, "seq")

    grads, own_mass, small = gradient(
        place, messages, columns, output_weight, hidden, falls, dp
    )
    parts = [grads[0]] + [swap(grads[k], "dp", k) for k in range(1, dp)]
    total, small = squares(small, parts)
    totals = [total] + [swap(total, "dp", k) for k in range(1, dp)]
    message = send_all(small, ("dp", "seq"), dp * seq)
    step_first, second, bias_step, bias, loss = scaled(
        place, message, totals, seq, model * units
    )
    return (
        own_mass.reshape(1, KEY_VALUE_HEADS, rows),
        loss[0, 0],
        step_first,
        second,
        bias_step.reshape(units),
        bias[:, 0],
    )


def solution(mesh):
    tokens = P("dp", "seq", None)
    return jax.shard_map(
        per_device,
        mesh=mesh,
        in_specs=(tokens, tokens, tokens, P(), P(), P(), P(), P()),
        out_specs=(P("dp", None, "seq"), P(), P("seq", None), P(), P(), P()),
        check_vma=False,
    )
```

```python
import functools

import jax
import jax.numpy as jnp
from jax import lax
from jax.experimental import pallas as pl
from jax.experimental.pallas import tpu as pltpu
from jax.sharding import PartitionSpec as P

KEY_VALUE_HEADS = 4
HEAD_SIZE = 128
BLK = 64
QUERY_GROUP_SIZE = 8
LOG2_E = 1.4426950408889634
VMEM_LIMIT = 60 * 1024 * 1024
VMEM = pl.BlockSpec(memory_space=pltpu.VMEM)
SMEM = pl.BlockSpec(memory_space=pltpu.SMEM)


def swap(value, axis, mask):
    return lax.ppermute(value, axis, [(i, i ^ mask) for i in range(lax.axis_size(axis))])


def gather_far(value, axis):
    top = lax.axis_size(axis) // 4
    return [value] + [swap(value, axis, step * top) for step in (1, 2, 3)]


def gather_even(far, axis):
    top = lax.axis_size(axis) // 4
    slots = {step * top: far[step] for step in range(4)}
    for mask in range(2, top, 2):
        for step in range(4):
            slots[step * top + mask] = swap(slots[step * top], axis, mask)
    return [slots[k] for k in range(0, 4 * top, 2)]


def gather_odd(even, axis):
    pairs = [(slot, swap(slot, axis, 1)) for slot in even]
    return [slot for pair in pairs for slot in pair]


def double(stacked, axis, mask):
    return jnp.concatenate([stacked, swap(stacked, axis, mask)], axis=0)


def near_order(amount):
    order = [(0, 0)]
    mask = amount // 4
    while mask > 1:
        order = order + [(0, at ^ mask) for _, at in order]
        mask //= 2
    return order + [(1, at) for _, at in order]


def pack(ref, value):
    rows = value.shape[0]
    reach = jnp.max(jnp.max(jnp.abs(value), axis=0, keepdims=True), axis=1, keepdims=True)
    power = jnp.ceil(jnp.log2(jnp.maximum(reach, 1e-30)))
    ref[:rows, :] = value * jnp.exp2(-power)
    ref[rows:, :] = jnp.broadcast_to(power, (ref.shape[0] - rows, value.shape[1]))


def unpack(ref):
    rows = ref.shape[0] - 16
    return ref[:rows, :] * jnp.exp2(ref[rows : rows + 1, :])


def halved(value):
    value = lax.reduce_precision(value, exponent_bits=5, mantissa_bits=10)
    return value, value.astype(jnp.float16)


def split3(value):
    high = value.astype(jnp.bfloat16)
    rest = value - high.astype(jnp.float32)
    middle = rest.astype(jnp.bfloat16)
    low = (rest - middle.astype(jnp.float32)).astype(jnp.bfloat16)
    return high, middle, low


def prepare_kernel(
    chunks,
    tokens_ref,
    weight_ref,
    bias_ref,
    output_ref,
    output_bias_ref,
    turned_ref,
    hidden_ref,
    fall_ref,
    predicted_ref,
    reach_ref,
    tokens,
    weight,
    turned,
    copied,
):
    rows = tokens.shape[1]
    block = tokens.shape[2]
    held = turned.shape[1]
    half = chunks // 2

    def copy_in(c):
        at = pl.ds(c * block, block)
        return (
            pltpu.make_async_copy(tokens_ref.at[:, at], tokens.at[c], copied.at[0, c]),
            pltpu.make_async_copy(weight_ref.at[at], weight.at[c], copied.at[1, c]),
        )

    def copy_out(c):
        at = turned_ref.at[pl.ds(c % half * held, held), c // half]
        return pltpu.make_async_copy(turned.at[c], at, copied.at[2, c])

    for c in range(chunks):
        for copy in copy_in(c):
            copy.start()
    pre_act = jnp.broadcast_to(bias_ref[...], hidden_ref.shape)
    for c in range(chunks):
        for copy in copy_in(c):
            copy.wait()
        part = tokens[c]
        turned[c] = jnp.transpose(part).reshape(turned.shape[1:])
        copy_out(c).start()
        pre_act = pre_act + jnp.dot(part, weight[c], preferred_element_type=jnp.float32)
    gate = jax.nn.sigmoid(pre_act)
    hidden = (pre_act * gate).astype(jnp.bfloat16)
    hidden_ref[...] = hidden
    predicted = lax.dot_general(
        output_ref[...], hidden, (((1,), (1,)), ((), ())), preferred_element_type=jnp.float32
    )
    for head in range(predicted.shape[0]):
        predicted_ref[head : head + 1, :] = predicted[head : head + 1] + output_bias_ref[head]
    fall = gate * (1.0 + pre_act * (1.0 - gate))
    reach = jnp.maximum(jnp.max(jnp.abs(fall), axis=1, keepdims=True), 1e-30)
    fall_ref[...] = fall / reach
    reach_ref[...] = jnp.transpose(jnp.broadcast_to(reach, (rows, rows)))[:1]
    for c in range(chunks):
        copy_out(c).wait()


def prepare(tokens, first_weight, first_bias, output_weight, output_bias, slots):
    rows, model = tokens.shape
    units = first_weight.shape[1]
    share = model // slots // 2
    block = max(share, min(1024, model // 2))
    chunks = model // block
    heads = output_weight.shape[0]
    anywhere = pl.BlockSpec(memory_space=pl.ANY)
    return pl.pallas_call(
        functools.partial(prepare_kernel, chunks),
        out_shape=(
            jax.ShapeDtypeStruct((slots, 2, share, rows), jnp.bfloat16),
            jax.ShapeDtypeStruct((rows, units), jnp.bfloat16),
            jax.ShapeDtypeStruct((rows, units), jnp.float32),
            jax.ShapeDtypeStruct((heads, rows), jnp.float32),
            jax.ShapeDtypeStruct((1, rows), jnp.float32),
        ),
        in_specs=[anywhere, anywhere, VMEM, VMEM, SMEM],
        out_specs=(anywhere, VMEM, VMEM, VMEM, VMEM),
        scratch_shapes=[
            pltpu.VMEM((chunks, rows, block), jnp.bfloat16),
            pltpu.VMEM((chunks, block, units), jnp.bfloat16),
            pltpu.VMEM((chunks, block // share, share, rows), jnp.bfloat16),
            pltpu.SemaphoreType.DMA((3, chunks)),
        ],
        compiler_params=pltpu.CompilerParams(vmem_limit_bytes=VMEM_LIMIT),
        cost_estimate=pl.CostEstimate(
            flops=2 * rows * model * units,
            bytes_accessed=2 * model * (units + 2 * rows),
            transcendentals=rows * units,
        ),
    )(tokens, first_weight, first_bias[None], output_weight, output_bias)


def attention_kernel(slots, heads, order_ref, query_ref, *refs):
    key_refs, mass_ref = refs[:slots], refs[-5]
    keys, bias, scores, mixed = refs[-4:]
    beside_refs = refs[slots:-5]
    rows = key_refs[0].shape[0]
    total = rows * slots
    lanes = scores.shape[1]
    fold = lanes // rows
    first, count = heads
    chunk = 256
    blocks = rows // BLK
    me = lax.axis_index("seq")
    scale = HEAD_SIZE ** (-0.5) * LOG2_E

    def pos_of(owner, index):
        at = jnp.zeros(index.shape, jnp.int32)
        for b in range(blocks):
            at = jnp.where(index // BLK == b, order_ref[owner * blocks + b], at)
        return at * BLK + index % BLK

    if beside_refs:
        early_ref, predicted_ref, reach_ref = beside_refs
        mass_ref[...] = jnp.zeros_like(mass_ref)
        mass_ref[:slots, :first, :] = early_ref[...]
        mass_ref[me, KEY_VALUE_HEADS:, :] = predicted_ref[...]
        beside = mass_ref.shape[0] - slots
        spot = lax.broadcasted_iota(jnp.int32, (beside, 8, rows), 0) * 8
        spot = spot + lax.broadcasted_iota(jnp.int32, (beside, 8, rows), 1)
        mass_ref[slots:] = jnp.where(spot == me, reach_ref[...][None], 0.0)
    query_pos = pos_of(me, lax.broadcasted_iota(jnp.int32, (rows, rows), 1))
    key_index = lax.broadcasted_iota(jnp.int32, (rows, rows), 0)
    for k in range(slots):
        at = pl.ds(k * rows, rows)
        for head in range(count):
            columns = slice((first + head) * HEAD_SIZE, (first + head + 1) * HEAD_SIZE)
            keys[head, at, :] = key_refs[k][:, columns]
        bias[at, :] = jnp.where(pos_of(me ^ k, key_index) <= query_pos, 0.0, -1e30)

    def visit_head(head, carried):
        mixed[...] = jnp.zeros_like(mixed)

        def visit_pair(pair, also):
            start = (first + head) * QUERY_GROUP_SIZE + pair * fold
            query = jnp.concatenate(
                [
                    query_ref[:, pl.ds(pl.multiple_of((start + j) * HEAD_SIZE, HEAD_SIZE), HEAD_SIZE)]
                    for j in range(fold)
                ],
                axis=0,
            )
            top = jnp.full((8, lanes), -1e30, jnp.float32)
            for c in range(total // chunk):
                at = pl.ds(c * chunk, chunk)
                raw = lax.dot_general(
                    keys[head, at, :],
                    query,
                    (((1,), (1,)), ((), ())),
                    preferred_element_type=jnp.float32,
                )
                shade = bias[at, :]
                raw = raw + jnp.concatenate([shade] * (lanes // rows), axis=1)
                scores[at, :] = raw
                top = jnp.maximum(top, jnp.max(raw.reshape(chunk // 8, 8, lanes), axis=0))
            top = jnp.max(top, axis=0, keepdims=True)
            summed = jnp.zeros((8, lanes), jnp.float32)
            for c in range(total // chunk):
                at = pl.ds(c * chunk, chunk)
                weight = jnp.exp2((scores[at, :] - top) * scale)
                scores[at, :] = weight
                summed = summed + jnp.sum(weight.reshape(chunk // 8, 8, lanes), axis=0)
            share = (1.0 / QUERY_GROUP_SIZE) / jnp.sum(summed, axis=0, keepdims=True)
            for c in range(total // chunk):
                at = pl.ds(c * chunk, chunk)
                part = scores[at, :] * share
                gathered = mixed[at, :]
                for j in range(lanes // rows):
                    gathered = gathered + part[:, j * rows : (j + 1) * rows]
                mixed[at, :] = gathered
            return also

        lax.fori_loop(0, QUERY_GROUP_SIZE // fold, visit_pair, 0)
        for k in range(slots):
            tile = jnp.transpose(mixed[pl.ds(k * rows, rows), :])
            row = jnp.sum(tile, axis=0, keepdims=True)
            mass_ref[me ^ k, pl.ds(head + (first if beside_refs else 0), 1), :] = row
        return carried

    lax.fori_loop(0, count, visit_head, 0)


def attention_mass(block_order, queries, key_slots, heads, beside=()):
    slots = len(key_slots)
    rows = key_slots[0].shape[0]
    total = rows * slots
    lanes = 2 * rows
    work = total * rows * heads[1] * QUERY_GROUP_SIZE
    if beside:
        shape = (slots + slots // 8, 8, rows)
    else:
        shape = (slots, heads[1], rows)
    return pl.pallas_call(
        functools.partial(attention_kernel, slots, heads),
        out_shape=jax.ShapeDtypeStruct(shape, jnp.float32),
        in_specs=[SMEM, VMEM] + [VMEM] * (slots + len(beside)),
        out_specs=VMEM,
        scratch_shapes=[
            pltpu.VMEM((heads[1], total, HEAD_SIZE), jnp.bfloat16),
            pltpu.VMEM((total, rows), jnp.float32),
            pltpu.VMEM((total, lanes), jnp.float32),
            pltpu.VMEM((total, rows), jnp.float32),
        ],
        compiler_params=pltpu.CompilerParams(vmem_limit_bytes=VMEM_LIMIT),
        cost_estimate=pl.CostEstimate(
            flops=20 * work * HEAD_SIZE, bytes_accessed=2 * queries.size, transcendentals=work
        ),
    )(block_order, queries, *key_slots, *beside)


def gradient_kernel(slots, columns_ref, output_ref, hidden_ref, *refs):
    message_refs, fall_refs = refs[:2], refs[2:4]
    keep_ref, send_ref, mass_ref, small_ref = refs[4:8]
    out_grad, slope, wide, grad, reaches = refs[8:]
    me, part = lax.axis_index("seq"), lax.axis_index("dp") % 2
    rows = hidden_ref.shape[0]
    total = rows * slots
    units = hidden_ref.shape[1]
    heads = KEY_VALUE_HEADS
    side = slots // 2
    sums = []
    for d in range(2):
        for k in range(slots):
            reaches[d, k] = message_refs[d][slots + k // 8, k % 8 : k % 8 + 1, :]
        mass = message_refs[d][:slots, :heads]
        residue = message_refs[d][:slots, heads:] - jnp.log(1.0 + mass)
        out_grad[d] = residue / total
        sums.append((jnp.sum(residue * residue), mass))
    loss_sum = sums[0][0] * (0.5 / total)
    mass_ref[...] = message_refs[0][me, :heads]
    grad_bias = jnp.sum(jnp.sum(out_grad[0], axis=0), axis=1, keepdims=True)
    output_rows = output_ref[...]
    output_three = jnp.concatenate([output_rows] * 3, axis=0)
    first_bias = jnp.zeros((8, units), jnp.float32)
    order = near_order(slots)
    for j in range(slots):
        d, mask = order[j // 2]
        mask = mask + j % 2
        scaled = out_grad[d, me ^ mask] * reaches[d, me ^ mask]
        back = lax.dot_general(
            jnp.concatenate(split3(scaled), axis=0),
            output_three,
            (((0,), (0,)), ((), ())),
            preferred_element_type=jnp.float32,
        )
        fall = back * fall_refs[j % 2][j // 2]
        first_bias = first_bias + jnp.sum(fall.reshape(rows // 8, 8, units), axis=0)
        at = slice(j * rows, (j + 1) * rows)
        slope[at, :] = fall.astype(jnp.bfloat16)
        wide[:, at] = columns_ref[2 * ((me ^ mask) % side) + (part ^ d)]
    grad[...] = jnp.dot(wide[...], slope[...], preferred_element_type=jnp.float32)
    share = keep_ref.shape[0]
    low = pl.multiple_of((me // side) * share, share)
    keep_ref[...] = grad[pl.ds(low, share), :]
    pack(send_ref, grad[pl.ds(pl.multiple_of(share - low, share), share), :])
    second = lax.dot_general(
        jnp.concatenate(split3(out_grad[0, me]), axis=0),
        hidden_ref[...],
        (((1,), (0,)), ((), ())),
        preferred_element_type=jnp.float32,
    )
    second = second[:heads] + second[heads : 2 * heads] + second[2 * heads :]
    lines = units // 128
    first_bias = jnp.sum(first_bias, axis=0, keepdims=True)
    small_ref[...] = jnp.zeros_like(small_ref)
    for c in range(lines):
        at = slice(c * 128, (c + 1) * 128)
        small_ref[pl.ds(c * heads, heads), :] = second[:, at]
        small_ref[pl.ds(lines * heads + c, 1), :] = first_bias[:, at]
    lane = lax.broadcasted_iota(jnp.int32, (1, 128), 1)
    last = jnp.where(lane == 0, loss_sum, 0.0)
    for head in range(heads):
        last = jnp.where(lane == 1 + head, grad_bias[head : head + 1], last)
    small_ref[pl.ds(lines * (heads + 1), 1), :] = last


def gradient(messages, columns, output_weight, hidden, falls):
    slots, depth, rows = columns.shape
    units = hidden.shape[1]
    return pl.pallas_call(
        functools.partial(gradient_kernel, slots),
        out_shape=(
            jax.ShapeDtypeStruct((depth // 2, units), jnp.float32),
            jax.ShapeDtypeStruct((depth // 2 + 16, units), jnp.float32),
            jax.ShapeDtypeStruct((KEY_VALUE_HEADS, rows), jnp.float32),
            jax.ShapeDtypeStruct((small_rows(units), 128), jnp.float32),
        ),
        in_specs=[VMEM] * 7,
        out_specs=(VMEM,) * 4,
        scratch_shapes=[
            pltpu.VMEM((2, slots, KEY_VALUE_HEADS, rows), jnp.float32),
            pltpu.VMEM((slots * rows, units), jnp.bfloat16),
            pltpu.VMEM((depth, slots * rows), jnp.bfloat16),
            pltpu.VMEM((depth, units), jnp.float32),
            pltpu.VMEM((2, slots, 1, rows), jnp.float32),
        ],
        compiler_params=pltpu.CompilerParams(vmem_limit_bytes=VMEM_LIMIT),
        cost_estimate=pl.CostEstimate(
            flops=2 * depth * slots * rows * units,
            bytes_accessed=2 * columns.size + 8 * slots * rows * units,
            transcendentals=0,
        ),
    )(columns, output_weight, hidden, *messages, *falls)


def small_rows(units):
    return -(-(units // 128 * (KEY_VALUE_HEADS + 1) + 1) // 8) * 8


def square_kernel(small_ref, keep_ref, other_ref, total_ref, send_ref):
    total = keep_ref[...] + unpack(other_ref)
    pack(total_ref, total)
    square = jnp.sum(jnp.sum(total * total, axis=0, keepdims=True), axis=1, keepdims=True)
    row = total.shape[1] // 128 * (KEY_VALUE_HEADS + 1)
    lane = lax.broadcasted_iota(jnp.int32, (1, 128), 1)
    send_ref[...] = small_ref[...]
    last = small_ref[pl.ds(row, 1), :]
    send_ref[pl.ds(row, 1), :] = jnp.where(lane == 1 + KEY_VALUE_HEADS, square, last)


def squares(small, keep, other):
    return pl.pallas_call(
        square_kernel,
        out_shape=(
            jax.ShapeDtypeStruct(other.shape, jnp.float32),
            jax.ShapeDtypeStruct(small.shape, jnp.float32),
        ),
        in_specs=[VMEM] * 3,
        out_specs=(VMEM, VMEM),
        compiler_params=pltpu.CompilerParams(vmem_limit_bytes=VMEM_LIMIT),
    )(small, keep, other)


def scale_kernel(slots, entries, message_ref, *refs):
    part_refs = refs[:2]
    step_ref, second_ref, first_bias_ref, bias_ref, loss_ref = refs[2:]
    part = lax.axis_index("dp") % 2
    devices = message_ref.shape[0]
    heads = KEY_VALUE_HEADS
    total = jnp.sum(message_ref[...], axis=0)
    once = message_ref[0]
    for d in range(slots, devices, slots):
        once = once + message_ref[d]
    twice = message_ref[0] + message_ref[slots // 2]
    for d in range(2 * slots, devices, 2 * slots):
        twice = twice + message_ref[d] + message_ref[d + slots // 2]
    lines = first_bias_ref.shape[1] // 128
    row = lines * (heads + 1)
    square = total[row : row + 1, 1 + heads : 2 + heads]
    inverse = 1.0 / jnp.sqrt(square / entries + 1e-06)
    share = part_refs[0].shape[0] - 16
    for k in range(2):
        at = pl.ds(pl.multiple_of((part ^ k) * share, share), share)
        step_ref[at, :] = unpack(part_refs[k]) * inverse

    def normal(piece):
        spread = jnp.sum(jnp.sum(piece * piece, axis=0, keepdims=True), axis=1, keepdims=True)
        return 1.0 / jnp.sqrt(spread / piece.size + 1e-06)

    second = total[: lines * heads]
    second = second * normal(second)
    first_bias = twice[lines * heads : row]
    first_bias = first_bias * normal(first_bias)
    for c in range(lines):
        at = slice(c * 128, (c + 1) * 128)
        second_ref[:, at] = second[c * heads : (c + 1) * heads]
        first_bias_ref[:, at] = first_bias[c : c + 1]
    last = once[row : row + 1]
    lane = lax.broadcasted_iota(jnp.int32, (1, 128), 1)
    loss_ref[0] = jnp.sum(jnp.where(lane == 0, last, 0.0))
    for head in range(heads):
        bias_ref[head] = jnp.sum(jnp.where(lane == 1 + head, last, 0.0))


def scaled(message, parts, slots, entries):
    share, units = parts[0].shape[0] - 16, parts[0].shape[1]
    return pl.pallas_call(
        functools.partial(scale_kernel, slots, entries),
        out_shape=(
            jax.ShapeDtypeStruct((2 * share, units), jnp.float32),
            jax.ShapeDtypeStruct((KEY_VALUE_HEADS, units), jnp.float32),
            jax.ShapeDtypeStruct((1, units), jnp.float32),
            jax.ShapeDtypeStruct((KEY_VALUE_HEADS,), jnp.float32),
            jax.ShapeDtypeStruct((1,), jnp.float32),
        ),
        in_specs=[VMEM] * 3,
        out_specs=(VMEM, VMEM, VMEM, SMEM, SMEM),
        compiler_params=pltpu.CompilerParams(vmem_limit_bytes=VMEM_LIMIT),
    )(message, *parts)


def send_all(value, axes, amount):
    copies = jnp.broadcast_to(value[None], (amount,) + value.shape)
    return lax.all_to_all(copies, axes, 0, 0, tiled=True)


def per_device(
    queries,
    rotated_key_rows,
    hidden_states,
    block_order,
    first_weight,
    first_bias,
    output_weight,
    output_bias,
):
    seq, dp = lax.axis_size("seq"), lax.axis_size("dp")
    rows, model = hidden_states.shape[1:]
    units = first_weight.shape[1]
    tokens = hidden_states.reshape(rows, model)

    key_far = gather_far(rotated_key_rows.reshape(rows, -1), "seq")
    turned, hidden, fall, predicted, reach = prepare(
        tokens, first_weight, first_bias, output_weight, output_bias, seq
    )
    key_even = gather_even(key_far, "seq")
    falls = fall.astype(jnp.float16)[None]
    mask = seq // 4
    while mask > 2:
        falls = double(falls, "seq", mask)
        mask //= 2
    turned, *key_even = lax.optimization_barrier((turned, *key_even))
    key_slots = gather_odd(key_even, "seq")

    side = seq // 2
    groups = [
        [(d + k) * seq + h * side + r for r in range(side) for k in range(2)]
        for d in range(0, dp, 2)
        for h in range(2)
    ]
    columns = lax.all_to_all(
        turned.reshape(seq, -1, rows), ("dp", "seq"), 0, 0, tiled=True, axis_index_groups=groups
    )
    late = queries.reshape(rows, -1)
    half = KEY_VALUE_HEADS // 2
    early = attention_mass(block_order, late, key_slots, (0, half))
    falls = double(falls, "seq", 2)
    early, late, falls = lax.optimization_barrier((early, late, falls))
    message = attention_mass(
        block_order, late, key_slots, (half, half), (early, predicted, reach)
    )
    falls = double(falls, "dp", 1)
    mask = 1
    while mask < seq // 4:
        message = message + swap(message, "seq", mask)
        mask *= 2
    messages = gather_far(message, "seq")
    message = (messages[0] + messages[1]) + (messages[2] + messages[3])
    message, falls = lax.optimization_barrier((message, falls))
    falls = [falls.astype(jnp.float32), swap(falls, "seq", 1).astype(jnp.float32)]

    keep, send, own_mass, small = gradient(
        (message, swap(message, "dp", 1)), columns, output_weight, hidden, falls
    )
    mask = 2
    while mask < dp:
        keep = keep + swap(keep, "dp", mask)
        send = send + swap(send, "dp", mask)
        mask *= 2
    other = swap(halved(send)[1], "seq", side).astype(jnp.float32)
    total, small = squares(small, keep, other)
    total, sent = halved(total)
    totals = [total, swap(sent, "dp", 1).astype(jnp.float32)]
    message = send_all(small, ("dp", "seq"), dp * seq)
    step_first, second, bias_step, bias, loss = scaled(
        message, totals, seq, model * units * (dp // 2)
    )
    return (
        own_mass.reshape(1, KEY_VALUE_HEADS, rows),
        loss.reshape(()),
        step_first,
        second,
        bias_step.reshape(units),
        bias,
    )


def solution(mesh):
    tokens = P("dp", "seq", None)
    return jax.shard_map(
        per_device,
        mesh=mesh,
        in_specs=(tokens, tokens, tokens, P(), P(), P(), P(), P()),
        out_specs=(P("dp", None, "seq"), P(), P("seq", None), P(), P(), P()),
        check_vma=False,
    )
```

```python
import functools

import jax
import jax.numpy as jnp
from jax import lax
from jax.experimental import pallas as pl
from jax.experimental.pallas import tpu as pltpu
from jax.sharding import PartitionSpec as P

KEY_VALUE_HEADS = 4
HEAD_SIZE = 128
BLK = 64
QUERY_GROUP_SIZE = 8
LOG2_E = 1.4426950408889634
PREDICTED_SCALE = 1.0 / 16.0
VMEM_LIMIT = 60 * 1024 * 1024
VMEM = pl.BlockSpec(memory_space=pltpu.VMEM)
SMEM = pl.BlockSpec(memory_space=pltpu.SMEM)


def swap(value, axis, mask):
    return lax.ppermute(value, axis, [(i, i ^ mask) for i in range(lax.axis_size(axis))])


def gather_far(value, axis):
    top = lax.axis_size(axis) // 4
    return [value] + [swap(value, axis, step * top) for step in (1, 2, 3)]


def gather_even(far, axis):
    top = lax.axis_size(axis) // 4
    slots = {step * top: far[step] for step in range(4)}
    for mask in range(2, top, 2):
        for step in range(4):
            slots[step * top + mask] = swap(slots[step * top], axis, mask)
    return [slots[k] for k in range(0, 4 * top, 2)]


def gather_odd(even, axis):
    pairs = [(slot, swap(slot, axis, 1)) for slot in even]
    return [slot for pair in pairs for slot in pair]


def near_order(amount):
    order = [0]
    mask = 2
    while mask < amount // 4:
        order = order + [at ^ mask for at in order]
        mask *= 2
    return [(d, at ^ far) for d in (0, 1) for far in (0, amount // 4) for at in order]


def gather_near(value):
    dp, seq = lax.axis_size("dp"), lax.axis_size("seq")
    slots = [value]
    mask = 2
    while mask < seq // 4:
        slots = slots + [swap(slot, "seq", mask) for slot in slots]
        mask *= 2
    stacked = jnp.stack(slots)
    gathered = [stacked]
    for d, at in ((0, seq // 4), (1, 0), (1, seq // 4)):
        pairs = [(i * seq + j, (i ^ d) * seq + (j ^ at)) for i in range(dp) for j in range(seq)]
        gathered.append(lax.ppermute(stacked, ("dp", "seq"), pairs))
    return gathered


def pack(ref, value):
    rows = value.shape[0]
    reach = jnp.max(jnp.max(jnp.abs(value), axis=0, keepdims=True), axis=1, keepdims=True)
    power = jnp.ceil(jnp.log2(jnp.maximum(reach, 1e-30)))
    ref[:rows, :] = value * jnp.exp2(-power)
    ref[rows:, :] = jnp.broadcast_to(power, (ref.shape[0] - rows, value.shape[1]))


def unpack(ref):
    rows = ref.shape[0] - 16
    return ref[:rows, :] * jnp.exp2(ref[rows : rows + 1, :])


def halved(value):
    value = lax.reduce_precision(value, exponent_bits=5, mantissa_bits=10)
    return value, value.astype(jnp.float16)


def split3(value):
    high = value.astype(jnp.bfloat16)
    rest = value - high.astype(jnp.float32)
    middle = rest.astype(jnp.bfloat16)
    low = (rest - middle.astype(jnp.float32)).astype(jnp.bfloat16)
    return high, middle, low


def prepare_kernel(
    chunks,
    tokens_ref,
    weight_ref,
    bias_ref,
    output_ref,
    output_bias_ref,
    turned_ref,
    hidden_ref,
    fall_ref,
    tokens,
    weight,
    turned,
    copied,
):
    rows = tokens.shape[1]
    block = tokens.shape[2]
    held = turned.shape[1]
    half = chunks // 2

    def copy_in(c):
        at = pl.ds(c * block, block)
        return (
            pltpu.make_async_copy(tokens_ref.at[:, at], tokens.at[c], copied.at[0, c]),
            pltpu.make_async_copy(weight_ref.at[at], weight.at[c], copied.at[1, c]),
        )

    def copy_out(c):
        at = turned_ref.at[pl.ds(c % half * held, held), c // half]
        return pltpu.make_async_copy(turned.at[c], at, copied.at[2, c])

    for c in range(chunks):
        for copy in copy_in(c):
            copy.start()
    pre_act = jnp.broadcast_to(bias_ref[...], hidden_ref.shape)
    for c in range(chunks):
        for copy in copy_in(c):
            copy.wait()
        part = tokens[c]
        turned[c] = jnp.transpose(part).reshape(turned.shape[1:])
        copy_out(c).start()
        pre_act = pre_act + jnp.dot(part, weight[c], preferred_element_type=jnp.float32)
    gate = jax.nn.sigmoid(pre_act)
    hidden = (pre_act * gate).astype(jnp.bfloat16)
    hidden_ref[...] = hidden
    predicted = lax.dot_general(
        output_ref[...], hidden, (((1,), (1,)), ((), ())), preferred_element_type=jnp.float32
    )
    heads = predicted.shape[0]
    head = lax.broadcasted_iota(jnp.int32, predicted.shape, 0)
    for k in range(heads):
        predicted = predicted + jnp.where(head == k, output_bias_ref[k], 0.0)
    fall = gate * (1.0 + pre_act * (1.0 - gate))
    reach = jnp.maximum(jnp.max(jnp.abs(fall), axis=1, keepdims=True), 1e-30)
    power = jnp.ceil(jnp.log2(reach))
    fall_ref[:rows, :] = fall * jnp.exp2(-power)
    fall_ref[rows:, :] = jnp.zeros((fall_ref.shape[0] - rows, fall.shape[1]), jnp.float32)
    for k, piece in enumerate(split3(predicted * PREDICTED_SCALE)):
        fall_ref[rows + k * heads : rows + (k + 1) * heads, :rows] = piece.astype(jnp.float32)
    power = jnp.transpose(jnp.broadcast_to(power, (rows, rows)))[:1]
    fall_ref[rows + 3 * heads : rows + 3 * heads + 1, :rows] = power
    for c in range(chunks):
        copy_out(c).wait()


def prepare(tokens, first_weight, first_bias, output_weight, output_bias, slots):
    rows, model = tokens.shape
    units = first_weight.shape[1]
    share = model // slots // 2
    block = max(share, min(1024, model // 2))
    chunks = model // block
    anywhere = pl.BlockSpec(memory_space=pl.ANY)
    return pl.pallas_call(
        functools.partial(prepare_kernel, chunks),
        out_shape=(
            jax.ShapeDtypeStruct((slots, 2, share, rows), jnp.bfloat16),
            jax.ShapeDtypeStruct((rows, units), jnp.bfloat16),
            jax.ShapeDtypeStruct((rows + 16, units), jnp.float32),
        ),
        in_specs=[anywhere, anywhere, VMEM, VMEM, SMEM],
        out_specs=(anywhere, VMEM, VMEM),
        scratch_shapes=[
            pltpu.VMEM((chunks, rows, block), jnp.bfloat16),
            pltpu.VMEM((chunks, block, units), jnp.bfloat16),
            pltpu.VMEM((chunks, block // share, share, rows), jnp.bfloat16),
            pltpu.SemaphoreType.DMA((3, chunks)),
        ],
        compiler_params=pltpu.CompilerParams(vmem_limit_bytes=VMEM_LIMIT),
        cost_estimate=pl.CostEstimate(
            flops=2 * rows * model * units,
            bytes_accessed=2 * model * (units + 2 * rows),
            transcendentals=rows * units,
        ),
    )(tokens, first_weight, first_bias[None], output_weight, output_bias)


def attention_kernel(slots, order_ref, query_ref, *refs):
    key_refs, mass_ref = refs[:slots], refs[slots]
    keys, bias, scores, shares = refs[slots + 1 :]
    rows = key_refs[0].shape[0]
    total = rows * slots
    lanes = scores.shape[2]
    fold = lanes // rows
    blocks = rows // BLK
    me = lax.axis_index("seq")
    scale = HEAD_SIZE ** (-0.5) * LOG2_E

    def pos_of(owner, index):
        at = jnp.zeros(index.shape, jnp.int32)
        for b in range(blocks):
            at = jnp.where(index // BLK == b, order_ref[owner * blocks + b], at)
        return at * BLK + index % BLK

    side = slots // 2
    query_pos = pos_of(me, lax.broadcasted_iota(jnp.int32, (rows, rows), 1))
    key_index = lax.broadcasted_iota(jnp.int32, (rows, rows), 0)
    for k in range(slots):
        at = pl.ds(k * rows, rows)
        for head in range(KEY_VALUE_HEADS):
            keys[head, at, :] = key_refs[k][:, head * HEAD_SIZE : (head + 1) * HEAD_SIZE]
        bias[at, :] = jnp.where(pos_of(me ^ k, key_index) <= query_pos, 0.0, -1e30)

    def visit_head(head, carried):
        def visit_pair(pair):
            start = head * QUERY_GROUP_SIZE + pair * fold
            query = jnp.concatenate(
                [
                    query_ref[:, pl.ds(pl.multiple_of((start + j) * HEAD_SIZE, HEAD_SIZE), HEAD_SIZE)]
                    for j in range(fold)
                ],
                axis=0,
            )
            query = jnp.transpose(query)
            tops, sums = [], []
            for k in range(slots):
                at = pl.ds(k * rows, rows)
                raw = lax.dot_general(
                    keys[head, at, :],
                    query,
                    (((1,), (0,)), ((), ())),
                    preferred_element_type=jnp.float32,
                )
                raw = (raw + jnp.concatenate([bias[at, :]] * fold, axis=1)).reshape(-1, 8, lanes)
                top = jnp.max(raw, axis=0)
                weight = jnp.exp2((raw - top[None]) * scale)
                scores[pair, at, :] = weight.reshape(rows, lanes)
                tops.append(top)
                sums.append(jnp.sum(weight, axis=0))
            best = functools.reduce(jnp.maximum, tops)
            best = jnp.max(best, axis=0, keepdims=True)
            parts = [jnp.exp2((top - best) * scale) for top in tops]
            summed = sum(part * one for part, one in zip(parts, sums))
            share = (1.0 / QUERY_GROUP_SIZE) / jnp.sum(summed, axis=0, keepdims=True)
            for k in range(slots):
                shares[pair, k] = parts[k] * share

        for pair in range(QUERY_GROUP_SIZE // fold):
            visit_pair(pair)
        for k in range(slots):
            tile = jnp.zeros((rows // 8, 8, rows), jnp.float32)
            for pair in range(QUERY_GROUP_SIZE // fold):
                part = scores[pair, pl.ds(k * rows, rows), :].reshape(rows // 8, 8, lanes)
                part = part * shares[pair, k][None]
                for j in range(fold):
                    tile = tile + part[:, :, j * rows : (j + 1) * rows]
            tile = jnp.transpose(tile.reshape(rows, rows))
            row = jnp.sum(tile, axis=0, keepdims=True)
            mass_ref[k // side, (me ^ k) % side, pl.ds(head, 1), :] = row
        return carried

    lax.fori_loop(0, KEY_VALUE_HEADS, visit_head, 0)


def attention_mass(block_order, queries, key_slots):
    slots = len(key_slots)
    rows = key_slots[0].shape[0]
    total = rows * slots
    lanes = 2 * rows
    work = total * rows * KEY_VALUE_HEADS * QUERY_GROUP_SIZE
    shape = (2, slots // 2, KEY_VALUE_HEADS, rows)
    return pl.pallas_call(
        functools.partial(attention_kernel, slots),
        out_shape=jax.ShapeDtypeStruct(shape, jnp.float32),
        in_specs=[SMEM] + [VMEM] * (slots + 1),
        out_specs=VMEM,
        scratch_shapes=[
            pltpu.VMEM((KEY_VALUE_HEADS, total, HEAD_SIZE), jnp.bfloat16),
            pltpu.VMEM((total, rows), jnp.float32),
            pltpu.VMEM((QUERY_GROUP_SIZE * rows // lanes, total, lanes), jnp.float32),
            pltpu.VMEM((QUERY_GROUP_SIZE * rows // lanes, slots, 8, lanes), jnp.float32),
        ],
        compiler_params=pltpu.CompilerParams(vmem_limit_bytes=VMEM_LIMIT),
        cost_estimate=pl.CostEstimate(
            flops=100 * work * HEAD_SIZE, bytes_accessed=2 * queries.size, transcendentals=work
        ),
    )(block_order, queries, *key_slots)


def gradient_kernel(slots, columns_ref, output_ref, hidden_ref, *refs):
    message_refs, fall_refs = refs[:2], refs[2:4]
    keep_ref, send_ref, mass_ref, small_ref = refs[4:8]
    slope, wide, grad = refs[8:]
    me, part = lax.axis_index("seq"), lax.axis_index("dp") % 2
    rows = hidden_ref.shape[0]
    total = rows * slots
    units = hidden_ref.shape[1]
    heads = KEY_VALUE_HEADS
    side = slots // 2
    mass_ref[...] = message_refs[0][me % side]
    output_rows = output_ref[...]
    output_three = jnp.concatenate([output_rows] * 3, axis=0)
    first_bias = jnp.zeros((8, units), jnp.float32)
    squared = jnp.zeros((heads, rows), jnp.float32)
    grad_bias = jnp.zeros((heads, rows), jnp.float32)
    order = near_order(slots)
    for j in range(slots):
        d, mask = order[j // 2]
        mask = mask + j % 2
        held = fall_refs[j % 2][j // 2]
        beside = held[rows:, :rows]
        predicted = (beside[:heads] + beside[heads : 2 * heads]) + beside[2 * heads : 3 * heads]
        mass = message_refs[d][(me ^ mask) % side]
        residue = predicted * (1.0 / PREDICTED_SCALE) - jnp.log(1.0 + mass)
        out_grad = residue / total
        if j == 0:
            own_grad = out_grad
        squared = squared + residue * residue
        grad_bias = grad_bias + out_grad
        scaled = out_grad * jnp.exp2(beside[3 * heads : 3 * heads + 1])
        back = lax.dot_general(
            jnp.concatenate(split3(scaled), axis=0),
            output_three,
            (((0,), (0,)), ((), ())),
            preferred_element_type=jnp.float32,
        )
        fall = back * held[:rows]
        first_bias = first_bias + jnp.sum(fall.reshape(rows // 8, 8, units), axis=0)
        at = slice(j * rows, (j + 1) * rows)
        slope[at, :] = fall.astype(jnp.bfloat16)
        wide[:, at] = columns_ref[2 * ((me ^ mask) % side) + (part ^ d)]
    loss_sum = jnp.sum(squared) * (0.5 / total)
    grad_bias = jnp.sum(grad_bias, axis=1, keepdims=True)
    grad[...] = jnp.dot(wide[...], slope[...], preferred_element_type=jnp.float32)
    share = keep_ref.shape[0]
    low = pl.multiple_of((me // side) * share, share)
    keep_ref[...] = grad[pl.ds(low, share), :]
    pack(send_ref, grad[pl.ds(pl.multiple_of(share - low, share), share), :])
    second = lax.dot_general(
        jnp.concatenate(split3(own_grad), axis=0),
        hidden_ref[...],
        (((1,), (0,)), ((), ())),
        preferred_element_type=jnp.float32,
    )
    second = second[:heads] + second[heads : 2 * heads] + second[2 * heads :]
    lines = units // 128
    first_bias = jnp.sum(first_bias, axis=0, keepdims=True)
    small_ref[...] = jnp.zeros_like(small_ref)
    for c in range(lines):
        at = slice(c * 128, (c + 1) * 128)
        small_ref[pl.ds(c * heads, heads), :] = second[:, at]
        small_ref[pl.ds(lines * heads + c, 1), :] = first_bias[:, at]
    lane = lax.broadcasted_iota(jnp.int32, (1, 128), 1)
    last = jnp.where(lane == 0, loss_sum, 0.0)
    for head in range(heads):
        last = jnp.where(lane == 1 + head, grad_bias[head : head + 1], last)
    small_ref[pl.ds(lines * (heads + 1), 1), :] = last


def gradient(messages, columns, output_weight, hidden, falls):
    slots, depth, rows = columns.shape
    units = hidden.shape[1]
    return pl.pallas_call(
        functools.partial(gradient_kernel, slots),
        out_shape=(
            jax.ShapeDtypeStruct((depth // 2, units), jnp.float32),
            jax.ShapeDtypeStruct((depth // 2 + 16, units), jnp.float32),
            jax.ShapeDtypeStruct((KEY_VALUE_HEADS, rows), jnp.float32),
            jax.ShapeDtypeStruct((small_rows(units), 128), jnp.float32),
        ),
        in_specs=[VMEM] * 7,
        out_specs=(VMEM,) * 4,
        scratch_shapes=[
            pltpu.VMEM((slots * rows, units), jnp.bfloat16),
            pltpu.VMEM((depth, slots * rows), jnp.bfloat16),
            pltpu.VMEM((depth, units), jnp.float32),
        ],
        compiler_params=pltpu.CompilerParams(vmem_limit_bytes=VMEM_LIMIT),
        cost_estimate=pl.CostEstimate(
            flops=2 * depth * slots * rows * units,
            bytes_accessed=2 * columns.size + 8 * slots * rows * units,
            transcendentals=0,
        ),
    )(columns, output_weight, hidden, *messages, *falls)


def small_rows(units):
    return -(-(units // 128 * (KEY_VALUE_HEADS + 1) + 1) // 8) * 8


def square_kernel(small_ref, keep_ref, other_ref, total_ref, send_ref):
    total = keep_ref[...] + unpack(other_ref)
    pack(total_ref, total)
    square = jnp.sum(jnp.sum(total * total, axis=0, keepdims=True), axis=1, keepdims=True)
    row = total.shape[1] // 128 * (KEY_VALUE_HEADS + 1)
    lane = lax.broadcasted_iota(jnp.int32, (1, 128), 1)
    last = jnp.where(lane == 1 + KEY_VALUE_HEADS, square, small_ref[row : row + 1, :])
    for k in range(send_ref.shape[0]):
        send_ref[k] = small_ref[...]
        send_ref[k, row : row + 1, :] = last


def squares(small, keep, other, devices):
    return pl.pallas_call(
        square_kernel,
        out_shape=(
            jax.ShapeDtypeStruct(other.shape, jnp.float32),
            jax.ShapeDtypeStruct((devices,) + small.shape, jnp.float32),
        ),
        in_specs=[VMEM] * 3,
        out_specs=(VMEM, VMEM),
        compiler_params=pltpu.CompilerParams(vmem_limit_bytes=VMEM_LIMIT),
    )(small, keep, other)


def scale_kernel(slots, entries, message_ref, *refs):
    part_refs = refs[:2]
    step_ref, second_ref, first_bias_ref, bias_ref, loss_ref = refs[2:]
    part = lax.axis_index("dp") % 2
    devices = message_ref.shape[0]
    heads = KEY_VALUE_HEADS
    total = jnp.sum(message_ref[...], axis=0)
    twice = message_ref[0] + message_ref[slots // 2]
    for d in range(2 * slots, devices, 2 * slots):
        twice = twice + message_ref[d] + message_ref[d + slots // 2]
    lines = first_bias_ref.shape[1] // 128
    row = lines * (heads + 1)
    square = total[row : row + 1, 1 + heads : 2 + heads]
    inverse = 1.0 / jnp.sqrt(square / entries + 1e-06)
    share = part_refs[0].shape[0] - 16
    for k in range(2):
        at = pl.ds(pl.multiple_of((part ^ k) * share, share), share)
        step_ref[at, :] = unpack(part_refs[k]) * inverse

    def normal(piece):
        spread = jnp.sum(jnp.sum(piece * piece, axis=0, keepdims=True), axis=1, keepdims=True)
        return 1.0 / jnp.sqrt(spread / piece.size + 1e-06)

    second = total[: lines * heads]
    second = second * normal(second)
    first_bias = twice[lines * heads : row]
    first_bias = first_bias * normal(first_bias)
    for c in range(lines):
        at = slice(c * 128, (c + 1) * 128)
        second_ref[:, at] = second[c * heads : (c + 1) * heads]
        first_bias_ref[:, at] = first_bias[c : c + 1]
    last = twice[row : row + 1]
    lane = lax.broadcasted_iota(jnp.int32, (1, 128), 1)
    loss_ref[0] = jnp.sum(jnp.where(lane == 0, last, 0.0))
    for head in range(heads):
        bias_ref[head] = jnp.sum(jnp.where(lane == 1 + head, last, 0.0))


def scaled(message, parts, slots, entries):
    share, units = parts[0].shape[0] - 16, parts[0].shape[1]
    return pl.pallas_call(
        functools.partial(scale_kernel, slots, entries),
        out_shape=(
            jax.ShapeDtypeStruct((2 * share, units), jnp.float32),
            jax.ShapeDtypeStruct((KEY_VALUE_HEADS, units), jnp.float32),
            jax.ShapeDtypeStruct((1, units), jnp.float32),
            jax.ShapeDtypeStruct((KEY_VALUE_HEADS,), jnp.float32),
            jax.ShapeDtypeStruct((1,), jnp.float32),
        ),
        in_specs=[VMEM] * 3,
        out_specs=(VMEM, VMEM, VMEM, SMEM, SMEM),
        compiler_params=pltpu.CompilerParams(vmem_limit_bytes=VMEM_LIMIT),
    )(message, *parts)


def per_device(
    queries,
    rotated_key_rows,
    hidden_states,
    block_order,
    first_weight,
    first_bias,
    output_weight,
    output_bias,
):
    seq, dp = lax.axis_size("seq"), lax.axis_size("dp")
    rows, model = hidden_states.shape[1:]
    units = first_weight.shape[1]
    tokens = hidden_states.reshape(rows, model)

    key_far = gather_far(rotated_key_rows.reshape(rows, -1), "seq")
    turned, hidden, falls = prepare(
        tokens, first_weight, first_bias, output_weight, output_bias, seq
    )
    falls, *far = lax.optimization_barrier((falls, *key_far[1:]))
    key_even = gather_even(key_far[:1] + far, "seq")
    falls = gather_near(falls.astype(jnp.float16))
    key_slots = gather_odd(key_even, "seq")
    turned, falls, *_ = lax.optimization_barrier((turned, falls, *key_even))

    side = seq // 2
    groups = [
        [(d + k) * seq + h * side + r for r in range(side) for k in range(2)]
        for d in range(0, dp, 2)
        for h in range(2)
    ]
    columns = lax.all_to_all(
        turned.reshape(seq, -1, rows), ("dp", "seq"), 0, 0, tiled=True, axis_index_groups=groups
    )
    message = attention_mass(block_order, queries.reshape(rows, -1), key_slots)
    message, *falls = lax.optimization_barrier((message, *falls))
    falls = jnp.concatenate(falls, axis=0)
    falls = [falls.astype(jnp.float32), swap(falls, "seq", 1).astype(jnp.float32)]
    mask = 1
    while mask < seq // 4:
        message = message + swap(message, "seq", mask)
        mask *= 2
    top = seq // 4
    message = (message[0] + swap(message[0], "seq", top)) + (
        swap(message[1], "seq", 2 * top) + swap(message[1], "seq", 3 * top)
    )
    keep, send, own_mass, small = gradient(
        (message, swap(message, "dp", 1)), columns, output_weight, hidden, falls
    )
    mask = 2
    while mask < dp:
        keep = keep + swap(keep, "dp", mask)
        send = send + swap(send, "dp", mask)
        mask *= 2
    other = swap(halved(send)[1], "seq", side).astype(jnp.float32)
    total, small = squares(small, keep, other, dp * seq)
    total, sent = halved(total)
    totals = [total, swap(sent, "dp", 1).astype(jnp.float32)]
    message = lax.all_to_all(small, ("dp", "seq"), 0, 0, tiled=True)
    step_first, second, bias_step, bias, loss = scaled(
        message, totals, seq, model * units * (dp // 2)
    )
    return (
        own_mass.reshape(1, KEY_VALUE_HEADS, rows),
        loss.reshape(()),
        step_first,
        second,
        bias_step.reshape(units),
        bias,
    )


def solution(mesh):
    tokens = P("dp", "seq", None)
    return jax.shard_map(
        per_device,
        mesh=mesh,
        in_specs=(tokens, tokens, tokens, P(), P(), P(), P(), P()),
        out_specs=(P("dp", None, "seq"), P(), P("seq", None), P(), P(), P()),
        check_vma=False,
    )
```

```python
import functools

import jax
import jax.numpy as jnp
from jax import lax
from jax.experimental import pallas as pl
from jax.experimental.pallas import tpu as pltpu
from jax.sharding import PartitionSpec as P

KEY_VALUE_HEADS = 4
HEAD_SIZE = 128
BLK = 64
QUERY_GROUP_SIZE = 8
LOG2_E = 1.4426950408889634
PREDICTED_SCALE = 1.0 / 16.0
VMEM_LIMIT = 60 * 1024 * 1024
VMEM = pl.BlockSpec(memory_space=pltpu.VMEM)
SMEM = pl.BlockSpec(memory_space=pltpu.SMEM)


def swap(value, axis, mask):
    return lax.ppermute(value, axis, [(i, i ^ mask) for i in range(lax.axis_size(axis))])


def far_groups(amount):
    top = amount // 4
    return [[0], [top], [2 * top, 3 * top]]


def key_masks(amount):
    masks = []
    for near in range(0, amount // 4, 2):
        for group in far_groups(amount):
            masks += [[mask ^ near for mask in group], [mask ^ near ^ 1 for mask in group]]
    return masks


def far_keys(value):
    top = lax.axis_size("seq") // 4
    return [swap(value, "seq", step * top) for step in (1, 2, 3)]


def key_stacks(value, far):
    stacks, arrived = [], []
    for near in range(0, lax.axis_size("seq") // 4, 2):
        for stack in (value[None], far[0][None], jnp.stack(far[1:])):
            if near:
                stack = swap(stack, "seq", near)
                arrived.append(stack)
            stacks += [stack, swap(stack, "seq", 1)]
    return stacks, arrived


def near_order(amount):
    order = [0]
    mask = 2
    while mask < amount // 4:
        order = order + [at ^ mask for at in order]
        mask *= 2
    return [(d, at ^ far) for d in (0, 1) for far in (0, amount // 4) for at in order]


def gather_near(value):
    dp, seq = lax.axis_size("dp"), lax.axis_size("seq")
    slots = [value]
    mask = 2
    while mask < seq // 4:
        slots = slots + [swap(slot, "seq", mask) for slot in slots]
        mask *= 2
    stacked = jnp.stack(slots)
    gathered = [stacked]
    for d, at in ((0, seq // 4), (1, 0), (1, seq // 4)):
        pairs = [(i * seq + j, (i ^ d) * seq + (j ^ at)) for i in range(dp) for j in range(seq)]
        gathered.append(lax.ppermute(stacked, ("dp", "seq"), pairs))
    return gathered


def pack(ref, value):
    rows = value.shape[0]
    reach = jnp.max(jnp.max(jnp.abs(value), axis=0, keepdims=True), axis=1, keepdims=True)
    power = jnp.ceil(jnp.log2(jnp.maximum(reach, 1e-30)))
    ref[:rows, :] = value * jnp.exp2(-power)
    ref[rows:, :] = jnp.broadcast_to(power, (ref.shape[0] - rows, value.shape[1]))


def unpack(ref):
    rows = ref.shape[0] - 16
    return ref[:rows, :] * jnp.exp2(ref[rows : rows + 1, :])


def halved(value):
    value = lax.reduce_precision(value, exponent_bits=5, mantissa_bits=10)
    return value, value.astype(jnp.float16)


def split3(value):
    high = value.astype(jnp.bfloat16)
    rest = value - high.astype(jnp.float32)
    middle = rest.astype(jnp.bfloat16)
    low = (rest - middle.astype(jnp.float32)).astype(jnp.bfloat16)
    return high, middle, low


def prepare_kernel(
    chunks,
    tokens_ref,
    weight_ref,
    bias_ref,
    output_ref,
    output_bias_ref,
    turned_ref,
    hidden_ref,
    fall_ref,
    tokens,
    weight,
    turned,
    copied,
):
    rows = tokens.shape[1]
    block = tokens.shape[2]
    held = turned.shape[1]
    half = chunks // 2

    def copy_in(c):
        at = pl.ds(c * block, block)
        return (
            pltpu.make_async_copy(tokens_ref.at[:, at], tokens.at[c], copied.at[0, c]),
            pltpu.make_async_copy(weight_ref.at[at], weight.at[c], copied.at[1, c]),
        )

    def copy_out(c):
        at = turned_ref.at[pl.ds(c % half * held, held), c // half]
        return pltpu.make_async_copy(turned.at[c], at, copied.at[2, c])

    for c in range(chunks):
        for copy in copy_in(c):
            copy.start()
    pre_act = jnp.broadcast_to(bias_ref[...], hidden_ref.shape)
    for c in range(chunks):
        for copy in copy_in(c):
            copy.wait()
        part = tokens[c]
        turned[c] = jnp.transpose(part).reshape(turned.shape[1:])
        copy_out(c).start()
        pre_act = pre_act + jnp.dot(part, weight[c], preferred_element_type=jnp.float32)
    gate = jax.nn.sigmoid(pre_act)
    hidden = (pre_act * gate).astype(jnp.bfloat16)
    hidden_ref[...] = hidden
    predicted = lax.dot_general(
        output_ref[...], hidden, (((1,), (1,)), ((), ())), preferred_element_type=jnp.float32
    )
    heads = predicted.shape[0]
    head = lax.broadcasted_iota(jnp.int32, predicted.shape, 0)
    for k in range(heads):
        predicted = predicted + jnp.where(head == k, output_bias_ref[k], 0.0)
    fall = gate * (1.0 + pre_act * (1.0 - gate))
    reach = jnp.maximum(jnp.max(jnp.abs(fall), axis=1, keepdims=True), 1e-30)
    power = jnp.ceil(jnp.log2(reach))
    fall_ref[:rows, :] = fall * jnp.exp2(-power)
    fall_ref[rows:, :] = jnp.zeros((fall_ref.shape[0] - rows, fall.shape[1]), jnp.float32)
    for k, piece in enumerate(split3(predicted * PREDICTED_SCALE)):
        fall_ref[rows + k * heads : rows + (k + 1) * heads, :rows] = piece.astype(jnp.float32)
    power = jnp.transpose(jnp.broadcast_to(power, (rows, rows)))[:1]
    fall_ref[rows + 3 * heads : rows + 3 * heads + 1, :rows] = power
    for c in range(chunks):
        copy_out(c).wait()


def prepare(tokens, first_weight, first_bias, output_weight, output_bias, slots):
    rows, model = tokens.shape
    units = first_weight.shape[1]
    share = model // slots // 2
    block = max(share, min(1024, model // 2))
    chunks = model // block
    anywhere = pl.BlockSpec(memory_space=pl.ANY)
    return pl.pallas_call(
        functools.partial(prepare_kernel, chunks),
        out_shape=(
            jax.ShapeDtypeStruct((slots, 2, share, rows), jnp.bfloat16),
            jax.ShapeDtypeStruct((rows, units), jnp.bfloat16),
            jax.ShapeDtypeStruct((rows + 16, units), jnp.float32),
        ),
        in_specs=[anywhere, anywhere, VMEM, VMEM, SMEM],
        out_specs=(anywhere, VMEM, VMEM),
        scratch_shapes=[
            pltpu.VMEM((chunks, rows, block), jnp.bfloat16),
            pltpu.VMEM((chunks, block, units), jnp.bfloat16),
            pltpu.VMEM((chunks, block // share, share, rows), jnp.bfloat16),
            pltpu.SemaphoreType.DMA((3, chunks)),
        ],
        compiler_params=pltpu.CompilerParams(vmem_limit_bytes=VMEM_LIMIT),
        cost_estimate=pl.CostEstimate(
            flops=2 * rows * model * units,
            bytes_accessed=2 * model * (units + 2 * rows),
            transcendentals=rows * units,
        ),
    )(tokens, first_weight, first_bias[None], output_weight, output_bias)


def attention_kernel(slots, order_ref, query_ref, *refs):
    masks = key_masks(slots)
    key_refs, mass_ref = refs[: len(masks)], refs[len(masks)]
    keys, bias, scores, shares = refs[len(masks) + 1 :]
    rows = query_ref.shape[0]
    from_slot = {mask: (i, j) for i, group in enumerate(masks) for j, mask in enumerate(group)}
    total = rows * slots
    lanes = scores.shape[2]
    fold = lanes // rows
    blocks = rows // BLK
    me = lax.axis_index("seq")
    scale = HEAD_SIZE ** (-0.5) * LOG2_E

    def pos_of(owner, index):
        at = jnp.zeros(index.shape, jnp.int32)
        for b in range(blocks):
            at = jnp.where(index // BLK == b, order_ref[owner * blocks + b], at)
        return at * BLK + index % BLK

    side = slots // 2
    query_pos = pos_of(me, lax.broadcasted_iota(jnp.int32, (rows, rows), 1))
    key_index = lax.broadcasted_iota(jnp.int32, (rows, rows), 0)
    for k in range(slots):
        at = pl.ds(k * rows, rows)
        for head in range(KEY_VALUE_HEADS):
            i, j = from_slot[k]
            keys[head, at, :] = key_refs[i][j, :, head * HEAD_SIZE : (head + 1) * HEAD_SIZE]
        bias[at, :] = jnp.where(pos_of(me ^ k, key_index) <= query_pos, 0.0, -1e30)

    def visit_head(head, carried):
        def visit_pair(pair):
            start = head * QUERY_GROUP_SIZE + pair * fold
            query = jnp.concatenate(
                [
                    query_ref[:, pl.ds(pl.multiple_of((start + j) * HEAD_SIZE, HEAD_SIZE), HEAD_SIZE)]
                    for j in range(fold)
                ],
                axis=0,
            )
            query = jnp.transpose(query)
            tops, sums = [], []
            for k in range(slots):
                at = pl.ds(k * rows, rows)
                raw = lax.dot_general(
                    keys[head, at, :],
                    query,
                    (((1,), (0,)), ((), ())),
                    preferred_element_type=jnp.float32,
                )
                raw = (raw + jnp.concatenate([bias[at, :]] * fold, axis=1)).reshape(-1, 8, lanes)
                top = jnp.max(raw, axis=0)
                weight = jnp.exp2((raw - top[None]) * scale)
                scores[pair, at, :] = weight.reshape(rows, lanes)
                tops.append(top)
                sums.append(jnp.sum(weight, axis=0))
            best = functools.reduce(jnp.maximum, tops)
            best = jnp.max(best, axis=0, keepdims=True)
            parts = [jnp.exp2((top - best) * scale) for top in tops]
            summed = sum(part * one for part, one in zip(parts, sums))
            share = (1.0 / QUERY_GROUP_SIZE) / jnp.sum(summed, axis=0, keepdims=True)
            for k in range(slots):
                shares[pair, k] = parts[k] * share

        for pair in range(QUERY_GROUP_SIZE // fold):
            visit_pair(pair)
        for k in range(slots):
            tile = jnp.zeros((rows // 8, 8, rows), jnp.float32)
            for pair in range(QUERY_GROUP_SIZE // fold):
                part = scores[pair, pl.ds(k * rows, rows), :].reshape(rows // 8, 8, lanes)
                part = part * shares[pair, k][None]
                for j in range(fold):
                    tile = tile + part[:, :, j * rows : (j + 1) * rows]
            tile = jnp.transpose(tile.reshape(rows, rows))
            row = jnp.sum(tile, axis=0, keepdims=True)
            mass_ref[k // side, (me ^ k) % side, pl.ds(head, 1), :] = row
        return carried

    lax.fori_loop(0, KEY_VALUE_HEADS, visit_head, 0)


def attention_mass(block_order, queries, stacks, slots):
    rows = queries.shape[0]
    total = rows * slots
    lanes = 2 * rows
    work = total * rows * KEY_VALUE_HEADS * QUERY_GROUP_SIZE
    shape = (2, slots // 2, KEY_VALUE_HEADS, rows)
    return pl.pallas_call(
        functools.partial(attention_kernel, slots),
        out_shape=jax.ShapeDtypeStruct(shape, jnp.float32),
        in_specs=[SMEM] + [VMEM] * (len(stacks) + 1),
        out_specs=VMEM,
        scratch_shapes=[
            pltpu.VMEM((KEY_VALUE_HEADS, total, HEAD_SIZE), jnp.bfloat16),
            pltpu.VMEM((total, rows), jnp.float32),
            pltpu.VMEM((QUERY_GROUP_SIZE * rows // lanes, total, lanes), jnp.float32),
            pltpu.VMEM((QUERY_GROUP_SIZE * rows // lanes, slots, 8, lanes), jnp.float32),
        ],
        compiler_params=pltpu.CompilerParams(vmem_limit_bytes=VMEM_LIMIT),
        cost_estimate=pl.CostEstimate(
            flops=100 * work * HEAD_SIZE, bytes_accessed=2 * queries.size, transcendentals=work
        ),
    )(block_order, queries, *stacks)


def gradient_kernel(slots, columns_ref, output_ref, hidden_ref, *refs):
    message_refs, fall_refs = refs[:2], refs[2:4]
    keep_ref, send_ref, mass_ref, small_ref = refs[4:8]
    slope, wide, grad = refs[8:]
    me, part = lax.axis_index("seq"), lax.axis_index("dp") % 2
    rows = hidden_ref.shape[0]
    total = rows * slots
    units = hidden_ref.shape[1]
    heads = KEY_VALUE_HEADS
    side = slots // 2
    mass_ref[...] = message_refs[0][me % side]
    output_rows = output_ref[...]
    output_three = jnp.concatenate([output_rows] * 3, axis=0)
    first_bias = jnp.zeros((8, units), jnp.float32)
    squared = jnp.zeros((heads, rows), jnp.float32)
    grad_bias = jnp.zeros((heads, rows), jnp.float32)
    order = near_order(slots)
    for j in range(slots):
        d, mask = order[j // 2]
        mask = mask + j % 2
        held = fall_refs[j % 2][j // 2]
        beside = held[rows:, :rows]
        predicted = (beside[:heads] + beside[heads : 2 * heads]) + beside[2 * heads : 3 * heads]
        mass = message_refs[d][(me ^ mask) % side]
        residue = predicted * (1.0 / PREDICTED_SCALE) - jnp.log(1.0 + mass)
        out_grad = residue / total
        if j == 0:
            own_grad = out_grad
        squared = squared + residue * residue
        grad_bias = grad_bias + out_grad
        scaled = out_grad * jnp.exp2(beside[3 * heads : 3 * heads + 1])
        back = lax.dot_general(
            jnp.concatenate(split3(scaled), axis=0),
            output_three,
            (((0,), (0,)), ((), ())),
            preferred_element_type=jnp.float32,
        )
        fall = back * held[:rows]
        first_bias = first_bias + jnp.sum(fall.reshape(rows // 8, 8, units), axis=0)
        at = slice(j * rows, (j + 1) * rows)
        slope[at, :] = fall.astype(jnp.bfloat16)
        wide[:, at] = columns_ref[2 * ((me ^ mask) % side) + (part ^ d)]
    loss_sum = jnp.sum(squared) * (0.5 / total)
    grad_bias = jnp.sum(grad_bias, axis=1, keepdims=True)
    grad[...] = jnp.dot(wide[...], slope[...], preferred_element_type=jnp.float32)
    share = keep_ref.shape[0]
    low = pl.multiple_of((me // side) * share, share)
    keep_ref[...] = grad[pl.ds(low, share), :]
    pack(send_ref, grad[pl.ds(pl.multiple_of(share - low, share), share), :])
    second = lax.dot_general(
        jnp.concatenate(split3(own_grad), axis=0),
        hidden_ref[...],
        (((1,), (0,)), ((), ())),
        preferred_element_type=jnp.float32,
    )
    second = second[:heads] + second[heads : 2 * heads] + second[2 * heads :]
    lines = units // 128
    first_bias = jnp.sum(first_bias, axis=0, keepdims=True)
    small_ref[...] = jnp.zeros_like(small_ref)
    for c in range(lines):
        at = slice(c * 128, (c + 1) * 128)
        small_ref[pl.ds(c * heads, heads), :] = second[:, at]
        small_ref[pl.ds(lines * heads + c, 1), :] = first_bias[:, at]
    lane = lax.broadcasted_iota(jnp.int32, (1, 128), 1)
    last = jnp.where(lane == 0, loss_sum, 0.0)
    for head in range(heads):
        last = jnp.where(lane == 1 + head, grad_bias[head : head + 1], last)
    small_ref[pl.ds(lines * (heads + 1), 1), :] = last


def gradient(messages, columns, output_weight, hidden, falls):
    slots, depth, rows = columns.shape
    units = hidden.shape[1]
    return pl.pallas_call(
        functools.partial(gradient_kernel, slots),
        out_shape=(
            jax.ShapeDtypeStruct((depth // 2, units), jnp.float32),
            jax.ShapeDtypeStruct((depth // 2 + 16, units), jnp.float32),
            jax.ShapeDtypeStruct((KEY_VALUE_HEADS, rows), jnp.float32),
            jax.ShapeDtypeStruct((small_rows(units), 128), jnp.float32),
        ),
        in_specs=[VMEM] * 7,
        out_specs=(VMEM,) * 4,
        scratch_shapes=[
            pltpu.VMEM((slots * rows, units), jnp.bfloat16),
            pltpu.VMEM((depth, slots * rows), jnp.bfloat16),
            pltpu.VMEM((depth, units), jnp.float32),
        ],
        compiler_params=pltpu.CompilerParams(vmem_limit_bytes=VMEM_LIMIT),
        cost_estimate=pl.CostEstimate(
            flops=2 * depth * slots * rows * units,
            bytes_accessed=2 * columns.size + 8 * slots * rows * units,
            transcendentals=0,
        ),
    )(columns, output_weight, hidden, *messages, *falls)


def small_rows(units):
    return -(-(units // 128 * (KEY_VALUE_HEADS + 1) + 1) // 8) * 8


def square_kernel(small_ref, keep_ref, other_ref, total_ref, send_ref):
    total = keep_ref[...] + unpack(other_ref)
    pack(total_ref, total)
    square = jnp.sum(jnp.sum(total * total, axis=0, keepdims=True), axis=1, keepdims=True)
    row = total.shape[1] // 128 * (KEY_VALUE_HEADS + 1)
    lane = lax.broadcasted_iota(jnp.int32, (1, 128), 1)
    last = jnp.where(lane == 1 + KEY_VALUE_HEADS, square, small_ref[row : row + 1, :])
    for k in range(send_ref.shape[0]):
        send_ref[k] = small_ref[...]
        send_ref[k, row : row + 1, :] = last


def squares(small, keep, other, devices):
    return pl.pallas_call(
        square_kernel,
        out_shape=(
            jax.ShapeDtypeStruct(other.shape, jnp.float32),
            jax.ShapeDtypeStruct((devices,) + small.shape, jnp.float32),
        ),
        in_specs=[VMEM] * 3,
        out_specs=(VMEM, VMEM),
        compiler_params=pltpu.CompilerParams(vmem_limit_bytes=VMEM_LIMIT),
    )(small, keep, other)


def scale_kernel(slots, entries, message_ref, *refs):
    part_refs = refs[:2]
    step_ref, second_ref, first_bias_ref, bias_ref, loss_ref = refs[2:]
    part = lax.axis_index("dp") % 2
    devices = message_ref.shape[0]
    heads = KEY_VALUE_HEADS
    total = jnp.sum(message_ref[...], axis=0)
    twice = message_ref[0] + message_ref[slots // 2]
    for d in range(2 * slots, devices, 2 * slots):
        twice = twice + message_ref[d] + message_ref[d + slots // 2]
    lines = first_bias_ref.shape[1] // 128
    row = lines * (heads + 1)
    square = total[row : row + 1, 1 + heads : 2 + heads]
    inverse = 1.0 / jnp.sqrt(square / entries + 1e-06)
    share = part_refs[0].shape[0] - 16
    for k in range(2):
        at = pl.ds(pl.multiple_of((part ^ k) * share, share), share)
        step_ref[at, :] = unpack(part_refs[k]) * inverse

    def normal(piece):
        spread = jnp.sum(jnp.sum(piece * piece, axis=0, keepdims=True), axis=1, keepdims=True)
        return 1.0 / jnp.sqrt(spread / piece.size + 1e-06)

    second = total[: lines * heads]
    second = second * normal(second)
    first_bias = twice[lines * heads : row]
    first_bias = first_bias * normal(first_bias)
    for c in range(lines):
        at = slice(c * 128, (c + 1) * 128)
        second_ref[:, at] = second[c * heads : (c + 1) * heads]
        first_bias_ref[:, at] = first_bias[c : c + 1]
    last = twice[row : row + 1]
    lane = lax.broadcasted_iota(jnp.int32, (1, 128), 1)
    loss_ref[0] = jnp.sum(jnp.where(lane == 0, last, 0.0))
    for head in range(heads):
        bias_ref[head] = jnp.sum(jnp.where(lane == 1 + head, last, 0.0))


def scaled(message, parts, slots, entries):
    share, units = parts[0].shape[0] - 16, parts[0].shape[1]
    return pl.pallas_call(
        functools.partial(scale_kernel, slots, entries),
        out_shape=(
            jax.ShapeDtypeStruct((2 * share, units), jnp.float32),
            jax.ShapeDtypeStruct((KEY_VALUE_HEADS, units), jnp.float32),
            jax.ShapeDtypeStruct((1, units), jnp.float32),
            jax.ShapeDtypeStruct((KEY_VALUE_HEADS,), jnp.float32),
            jax.ShapeDtypeStruct((1,), jnp.float32),
        ),
        in_specs=[VMEM] * 3,
        out_specs=(VMEM, VMEM, VMEM, SMEM, SMEM),
        compiler_params=pltpu.CompilerParams(vmem_limit_bytes=VMEM_LIMIT),
    )(message, *parts)


def per_device(
    queries,
    rotated_key_rows,
    hidden_states,
    block_order,
    first_weight,
    first_bias,
    output_weight,
    output_bias,
):
    seq, dp = lax.axis_size("seq"), lax.axis_size("dp")
    rows, model = hidden_states.shape[1:]
    units = first_weight.shape[1]
    tokens = hidden_states.reshape(rows, model)

    keys = rotated_key_rows.reshape(rows, -1)
    far = far_keys(keys)
    turned, hidden, falls = prepare(
        tokens, first_weight, first_bias, output_weight, output_bias, seq
    )
    falls, *far = lax.optimization_barrier((falls, *far))
    stacks, arrived = key_stacks(keys, far)
    falls = gather_near(falls.astype(jnp.float16))
    turned, _ = lax.optimization_barrier((turned, arrived[1]))

    side = seq // 2
    groups = [
        [(d + k) * seq + h * side + r for r in range(side) for k in range(2)]
        for d in range(0, dp, 2)
        for h in range(2)
    ]
    columns = lax.all_to_all(
        turned.reshape(seq, -1, rows), ("dp", "seq"), 0, 0, tiled=True, axis_index_groups=groups
    )
    front, *falls = lax.optimization_barrier((queries.reshape(rows, -1), *falls))
    message = attention_mass(block_order, front, stacks, seq)
    message, *falls = lax.optimization_barrier((message, *falls))
    falls = jnp.concatenate(falls, axis=0)
    falls = [falls.astype(jnp.float32), swap(falls, "seq", 1).astype(jnp.float32)]
    message = message + swap(message, "seq", 1)
    mask = 2
    while mask < seq // 4:
        other, *falls = lax.optimization_barrier((swap(message, "seq", mask), *falls))
        message = message + other
        mask *= 2
    top = seq // 4
    message = (message[0] + swap(message[0], "seq", top)) + (
        swap(message[1], "seq", 2 * top) + swap(message[1], "seq", 3 * top)
    )
    keep, send, own_mass, small = gradient(
        (message, swap(message, "dp", 1)), columns, output_weight, hidden, falls
    )
    mask = 2
    while mask < dp:
        keep = keep + swap(keep, "dp", mask)
        send = send + swap(send, "dp", mask)
        mask *= 2
    other = swap(halved(send)[1], "seq", side).astype(jnp.float32)
    total, small = squares(small, keep, other, dp * seq)
    sent, total = lax.optimization_barrier((halved(total)[1], total))
    totals = [halved(total)[0], swap(sent, "dp", 1).astype(jnp.float32)]
    message = lax.all_to_all(small, ("dp", "seq"), 0, 0, tiled=True)
    step_first, second, bias_step, bias, loss = scaled(
        message, totals, seq, model * units * (dp // 2)
    )
    return (
        own_mass.reshape(1, KEY_VALUE_HEADS, rows),
        loss.reshape(()),
        step_first,
        second,
        bias_step.reshape(units),
        bias,
    )


def solution(mesh):
    tokens = P("dp", "seq", None)
    return jax.shard_map(
        per_device,
        mesh=mesh,
        in_specs=(tokens, tokens, tokens, P(), P(), P(), P(), P()),
        out_specs=(P("dp", None, "seq"), P(), P("seq", None), P(), P(), P()),
        check_vma=False,
    )
```

```python
import functools

import jax
import jax.numpy as jnp
from jax import lax
from jax.experimental import pallas as pl
from jax.experimental.pallas import tpu as pltpu
from jax.sharding import PartitionSpec as P

KEY_VALUE_HEADS = 4
HEAD_SIZE = 128
BLK = 64
QUERY_GROUP_SIZE = 8
LOG2_E = 1.4426950408889634
PREDICTED_SCALE = 1.0 / 16.0
VMEM_LIMIT = 40 * 1024 * 1024
PREPARE_VMEM_LIMIT = 60 * 1024 * 1024
VMEM = pl.BlockSpec(memory_space=pltpu.VMEM)
SMEM = pl.BlockSpec(memory_space=pltpu.SMEM)


def swap(value, axis, mask):
    return lax.ppermute(value, axis, [(i, i ^ mask) for i in range(lax.axis_size(axis))])


def far_groups(amount):
    top = amount // 4
    return [[0], [top], [2 * top, 3 * top]]


def key_masks(amount):
    masks = []
    for near in range(0, amount // 4, 2):
        for group in far_groups(amount):
            masks += [[mask ^ near for mask in group], [mask ^ near ^ 1 for mask in group]]
    return masks


def far_keys(value):
    top = lax.axis_size("seq") // 4
    return [swap(value, "seq", step * top) for step in (1, 2, 3)]


def key_stacks(value, far):
    stacks, arrived = [], []
    for near in range(0, lax.axis_size("seq") // 4, 2):
        for stack in (value[None], far[0][None], jnp.stack(far[1:])):
            if near:
                stack = swap(stack, "seq", near)
                arrived.append(stack)
            stacks += [stack, swap(stack, "seq", 1)]
    return stacks, arrived


def near_order(amount):
    order = [0]
    mask = 2
    while mask < amount // 4:
        order = order + [at ^ mask for at in order]
        mask *= 2
    return [(d, at ^ far) for d in (0, 1) for far in (0, amount // 4) for at in order]


def gather_near(value):
    dp, seq = lax.axis_size("dp"), lax.axis_size("seq")
    slots = [value]
    mask = 2
    while mask < seq // 4:
        slots = slots + [swap(slot, "seq", mask) for slot in slots]
        mask *= 2
    stacked = jnp.stack(slots)
    gathered = [stacked]
    for d, at in ((0, seq // 4), (1, 0), (1, seq // 4)):
        pairs = [(i * seq + j, (i ^ d) * seq + (j ^ at)) for i in range(dp) for j in range(seq)]
        gathered.append(lax.ppermute(stacked, ("dp", "seq"), pairs))
    return gathered


def pack(ref, value):
    rows = value.shape[0]
    reach = jnp.max(jnp.max(jnp.abs(value), axis=0, keepdims=True), axis=1, keepdims=True)
    power = jnp.ceil(jnp.log2(jnp.maximum(reach, 1e-30)))
    ref[:rows, :] = value * jnp.exp2(-power)
    ref[rows:, :] = jnp.broadcast_to(power, (ref.shape[0] - rows, value.shape[1]))


def unpack(ref):
    rows = ref.shape[0] - 16
    return ref[:rows, :] * jnp.exp2(ref[rows : rows + 1, :])


def halved(value):
    value = lax.reduce_precision(value, exponent_bits=5, mantissa_bits=10)
    return value, value.astype(jnp.float16)


def split3(value):
    high = value.astype(jnp.bfloat16)
    rest = value - high.astype(jnp.float32)
    middle = rest.astype(jnp.bfloat16)
    low = (rest - middle.astype(jnp.float32)).astype(jnp.bfloat16)
    return high, middle, low


def prepare_kernel(
    chunks,
    tokens_ref,
    weight_ref,
    bias_ref,
    output_ref,
    output_bias_ref,
    turned_ref,
    hidden_ref,
    fall_ref,
    tokens,
    weight,
    turned,
    copied,
):
    rows = tokens.shape[1]
    block = tokens.shape[2]
    held = turned.shape[1]
    half = chunks // 2

    def copy_in(c):
        at = pl.ds(c * block, block)
        return (
            pltpu.make_async_copy(tokens_ref.at[:, at], tokens.at[c], copied.at[0, c]),
            pltpu.make_async_copy(weight_ref.at[at], weight.at[c], copied.at[1, c]),
        )

    def copy_out(c):
        at = turned_ref.at[pl.ds(c % half * held, held), c // half]
        return pltpu.make_async_copy(turned.at[c], at, copied.at[2, c])

    for c in range(chunks):
        for copy in copy_in(c):
            copy.start()
    pre_act = jnp.broadcast_to(bias_ref[...], hidden_ref.shape)
    for c in range(chunks):
        for copy in copy_in(c):
            copy.wait()
        part = tokens[c]
        turned[c] = jnp.transpose(part).reshape(turned.shape[1:])
        copy_out(c).start()
        pre_act = pre_act + jnp.dot(part, weight[c], preferred_element_type=jnp.float32)
    gate = jax.nn.sigmoid(pre_act)
    hidden = (pre_act * gate).astype(jnp.bfloat16)
    hidden_ref[...] = hidden
    predicted = lax.dot_general(
        output_ref[...], hidden, (((1,), (1,)), ((), ())), preferred_element_type=jnp.float32
    )
    heads = predicted.shape[0]
    head = lax.broadcasted_iota(jnp.int32, predicted.shape, 0)
    for k in range(heads):
        predicted = predicted + jnp.where(head == k, output_bias_ref[k], 0.0)
    fall = gate * (1.0 + pre_act * (1.0 - gate))
    reach = jnp.maximum(jnp.max(jnp.abs(fall), axis=1, keepdims=True), 1e-30)
    power = jnp.ceil(jnp.log2(reach))
    fall_ref[:rows, :] = fall * jnp.exp2(-power)
    fall_ref[rows:, :] = jnp.zeros((fall_ref.shape[0] - rows, fall.shape[1]), jnp.float32)
    for k, piece in enumerate(split3(predicted * PREDICTED_SCALE)):
        fall_ref[rows + k * heads : rows + (k + 1) * heads, :rows] = piece.astype(jnp.float32)
    power = jnp.transpose(jnp.broadcast_to(power, (rows, rows)))[:1]
    fall_ref[rows + 3 * heads : rows + 3 * heads + 1, :rows] = power
    for c in range(chunks):
        copy_out(c).wait()


def prepare(tokens, first_weight, first_bias, output_weight, output_bias, slots):
    rows, model = tokens.shape
    units = first_weight.shape[1]
    share = model // slots // 2
    block = max(share, min(1024, model // 2))
    chunks = model // block
    anywhere = pl.BlockSpec(memory_space=pl.ANY)
    return pl.pallas_call(
        functools.partial(prepare_kernel, chunks),
        out_shape=(
            jax.ShapeDtypeStruct((slots, 2, share, rows), jnp.bfloat16),
            jax.ShapeDtypeStruct((rows, units), jnp.bfloat16),
            jax.ShapeDtypeStruct((rows + 16, units), jnp.float32),
        ),
        in_specs=[anywhere, anywhere, VMEM, VMEM, SMEM],
        out_specs=(anywhere, VMEM, VMEM),
        scratch_shapes=[
            pltpu.VMEM((chunks, rows, block), jnp.bfloat16),
            pltpu.VMEM((chunks, block, units), jnp.bfloat16),
            pltpu.VMEM((chunks, block // share, share, rows), jnp.bfloat16),
            pltpu.SemaphoreType.DMA((3, chunks)),
        ],
        compiler_params=pltpu.CompilerParams(vmem_limit_bytes=PREPARE_VMEM_LIMIT),
        cost_estimate=pl.CostEstimate(
            flops=2 * rows * model * units,
            bytes_accessed=2 * model * (units + 2 * rows),
            transcendentals=rows * units,
        ),
    )(tokens, first_weight, first_bias[None], output_weight, output_bias)


def attention_kernel(slots, order_ref, query_ref, *refs):
    masks = key_masks(slots)
    key_refs, mass_ref = refs[: len(masks)], refs[len(masks)]
    keys, bias, scores, shares = refs[len(masks) + 1 :]
    rows = query_ref.shape[0]
    from_slot = {mask: (i, j) for i, group in enumerate(masks) for j, mask in enumerate(group)}
    total = rows * slots
    lanes = scores.shape[2]
    fold = lanes // rows
    blocks = rows // BLK
    me = lax.axis_index("seq")
    scale = HEAD_SIZE ** (-0.5) * LOG2_E

    def pos_of(owner, index):
        at = jnp.zeros(index.shape, jnp.int32)
        for b in range(blocks):
            at = jnp.where(index // BLK == b, order_ref[owner * blocks + b], at)
        return at * BLK + index % BLK

    side = slots // 2
    query_pos = pos_of(me, lax.broadcasted_iota(jnp.int32, (rows, rows), 1))
    key_index = lax.broadcasted_iota(jnp.int32, (rows, rows), 0)
    for k in range(slots):
        at = pl.ds(k * rows, rows)
        for head in range(KEY_VALUE_HEADS):
            i, j = from_slot[k]
            keys[head, at, :] = key_refs[i][j, :, head * HEAD_SIZE : (head + 1) * HEAD_SIZE]
        bias[at, :] = jnp.where(pos_of(me ^ k, key_index) <= query_pos, 0.0, -1e30)

    def visit_head(head, carried):
        def visit_pair(pair):
            start = head * QUERY_GROUP_SIZE + pair * fold
            query = jnp.concatenate(
                [
                    query_ref[:, pl.ds(pl.multiple_of((start + j) * HEAD_SIZE, HEAD_SIZE), HEAD_SIZE)]
                    for j in range(fold)
                ],
                axis=0,
            )
            query = jnp.transpose(query)
            tops, sums = [], []
            for k in range(slots):
                at = pl.ds(k * rows, rows)
                raw = lax.dot_general(
                    keys[head, at, :],
                    query,
                    (((1,), (0,)), ((), ())),
                    preferred_element_type=jnp.float32,
                )
                raw = (raw + jnp.concatenate([bias[at, :]] * fold, axis=1)).reshape(-1, 8, lanes)
                top = jnp.max(raw, axis=0)
                weight = jnp.exp2((raw - top[None]) * scale)
                scores[pair, at, :] = weight.reshape(rows, lanes)
                tops.append(top)
                sums.append(jnp.sum(weight, axis=0))
            best = functools.reduce(jnp.maximum, tops)
            best = jnp.max(best, axis=0, keepdims=True)
            parts = [jnp.exp2((top - best) * scale) for top in tops]
            summed = sum(part * one for part, one in zip(parts, sums))
            share = (1.0 / QUERY_GROUP_SIZE) / jnp.sum(summed, axis=0, keepdims=True)
            for k in range(slots):
                shares[pair, k] = parts[k] * share

        for pair in range(QUERY_GROUP_SIZE // fold):
            visit_pair(pair)
        for k in range(slots):
            tile = jnp.zeros((rows // 8, 8, rows), jnp.float32)
            for pair in range(QUERY_GROUP_SIZE // fold):
                part = scores[pair, pl.ds(k * rows, rows), :].reshape(rows // 8, 8, lanes)
                part = part * shares[pair, k][None]
                for j in range(fold):
                    tile = tile + part[:, :, j * rows : (j + 1) * rows]
            tile = jnp.transpose(tile.reshape(rows, rows))
            row = jnp.sum(tile, axis=0, keepdims=True)
            mass_ref[k // side, (me ^ k) % side, pl.ds(head, 1), :] = row
        return carried

    lax.fori_loop(0, KEY_VALUE_HEADS, visit_head, 0)


def attention_mass(block_order, queries, stacks, slots):
    rows = queries.shape[0]
    total = rows * slots
    lanes = 2 * rows
    work = total * rows * KEY_VALUE_HEADS * QUERY_GROUP_SIZE
    shape = (2, slots // 2, KEY_VALUE_HEADS, rows)
    return pl.pallas_call(
        functools.partial(attention_kernel, slots),
        out_shape=jax.ShapeDtypeStruct(shape, jnp.float32),
        in_specs=[SMEM] + [VMEM] * (len(stacks) + 1),
        out_specs=VMEM,
        scratch_shapes=[
            pltpu.VMEM((KEY_VALUE_HEADS, total, HEAD_SIZE), jnp.bfloat16),
            pltpu.VMEM((total, rows), jnp.float32),
            pltpu.VMEM((QUERY_GROUP_SIZE * rows // lanes, total, lanes), jnp.float32),
            pltpu.VMEM((QUERY_GROUP_SIZE * rows // lanes, slots, 8, lanes), jnp.float32),
        ],
        compiler_params=pltpu.CompilerParams(vmem_limit_bytes=VMEM_LIMIT),
        cost_estimate=pl.CostEstimate(
            flops=100 * work * HEAD_SIZE, bytes_accessed=2 * queries.size, transcendentals=work
        ),
    )(block_order, queries, *stacks)


def gradient_kernel(slots, columns_ref, output_ref, hidden_ref, *refs):
    message_refs, fall_refs = refs[:2], refs[2:4]
    keep_ref, send_ref, mass_ref, small_ref = refs[4:8]
    slope, wide, grad = refs[8:]
    me, part = lax.axis_index("seq"), lax.axis_index("dp") % 2
    rows = hidden_ref.shape[0]
    total = rows * slots
    units = hidden_ref.shape[1]
    heads = KEY_VALUE_HEADS
    side = slots // 2
    mass_ref[...] = message_refs[0][me % side]
    output_rows = output_ref[...]
    output_three = jnp.concatenate([output_rows] * 3, axis=0)
    first_bias = jnp.zeros((8, units), jnp.float32)
    squared = jnp.zeros((heads, rows), jnp.float32)
    grad_bias = jnp.zeros((heads, rows), jnp.float32)
    order = near_order(slots)
    for j in range(slots):
        d, mask = order[j // 2]
        mask = mask + j % 2
        held = fall_refs[j % 2][j // 2]
        beside = held[rows:, :rows]
        predicted = (beside[:heads] + beside[heads : 2 * heads]) + beside[2 * heads : 3 * heads]
        mass = message_refs[d][(me ^ mask) % side]
        residue = predicted * (1.0 / PREDICTED_SCALE) - jnp.log(1.0 + mass)
        out_grad = residue / total
        if j == 0:
            own_grad = out_grad
        squared = squared + residue * residue
        grad_bias = grad_bias + out_grad
        scaled = out_grad * jnp.exp2(beside[3 * heads : 3 * heads + 1])
        back = lax.dot_general(
            jnp.concatenate(split3(scaled), axis=0),
            output_three,
            (((0,), (0,)), ((), ())),
            preferred_element_type=jnp.float32,
        )
        fall = back * held[:rows]
        first_bias = first_bias + jnp.sum(fall.reshape(rows // 8, 8, units), axis=0)
        at = slice(j * rows, (j + 1) * rows)
        slope[at, :] = fall.astype(jnp.bfloat16)
        wide[:, at] = columns_ref[2 * ((me ^ mask) % side) + (part ^ d)]
    loss_sum = jnp.sum(squared) * (0.5 / total)
    grad_bias = jnp.sum(grad_bias, axis=1, keepdims=True)
    grad[...] = jnp.dot(wide[...], slope[...], preferred_element_type=jnp.float32)
    share = keep_ref.shape[0]
    low = pl.multiple_of((me // side) * share, share)
    keep_ref[...] = grad[pl.ds(low, share), :]
    pack(send_ref, grad[pl.ds(pl.multiple_of(share - low, share), share), :])
    second = lax.dot_general(
        jnp.concatenate(split3(own_grad), axis=0),
        hidden_ref[...],
        (((1,), (0,)), ((), ())),
        preferred_element_type=jnp.float32,
    )
    second = second[:heads] + second[heads : 2 * heads] + second[2 * heads :]
    lines = units // 128
    first_bias = jnp.sum(first_bias, axis=0, keepdims=True)
    small_ref[...] = jnp.zeros_like(small_ref)
    for c in range(lines):
        at = slice(c * 128, (c + 1) * 128)
        small_ref[pl.ds(c * heads, heads), :] = second[:, at]
        small_ref[pl.ds(lines * heads + c, 1), :] = first_bias[:, at]
    lane = lax.broadcasted_iota(jnp.int32, (1, 128), 1)
    last = jnp.where(lane == 0, loss_sum, 0.0)
    for head in range(heads):
        last = jnp.where(lane == 1 + head, grad_bias[head : head + 1], last)
    small_ref[pl.ds(lines * (heads + 1), 1), :] = last


def gradient(messages, columns, output_weight, hidden, falls):
    slots, depth, rows = columns.shape
    units = hidden.shape[1]
    return pl.pallas_call(
        functools.partial(gradient_kernel, slots),
        out_shape=(
            jax.ShapeDtypeStruct((depth // 2, units), jnp.float32),
            jax.ShapeDtypeStruct((depth // 2 + 16, units), jnp.float32),
            jax.ShapeDtypeStruct((KEY_VALUE_HEADS, rows), jnp.float32),
            jax.ShapeDtypeStruct((small_rows(units), 128), jnp.float32),
        ),
        in_specs=[VMEM] * 7,
        out_specs=(VMEM,) * 4,
        scratch_shapes=[
            pltpu.VMEM((slots * rows, units), jnp.bfloat16),
            pltpu.VMEM((depth, slots * rows), jnp.bfloat16),
            pltpu.VMEM((depth, units), jnp.float32),
        ],
        compiler_params=pltpu.CompilerParams(vmem_limit_bytes=VMEM_LIMIT),
        cost_estimate=pl.CostEstimate(
            flops=2 * depth * slots * rows * units,
            bytes_accessed=2 * columns.size + 8 * slots * rows * units,
            transcendentals=0,
        ),
    )(columns, output_weight, hidden, *messages, *falls)


def small_rows(units):
    return -(-(units // 128 * (KEY_VALUE_HEADS + 1) + 1) // 8) * 8


def square_kernel(small_ref, keep_ref, other_ref, total_ref, send_ref):
    total = keep_ref[...] + unpack(other_ref)
    pack(total_ref, total)
    square = jnp.sum(jnp.sum(total * total, axis=0, keepdims=True), axis=1, keepdims=True)
    row = total.shape[1] // 128 * (KEY_VALUE_HEADS + 1)
    lane = lax.broadcasted_iota(jnp.int32, (1, 128), 1)
    last = jnp.where(lane == 1 + KEY_VALUE_HEADS, square, small_ref[row : row + 1, :])
    for k in range(send_ref.shape[0]):
        send_ref[k] = small_ref[...]
        send_ref[k, row : row + 1, :] = last


def squares(small, keep, other, devices):
    return pl.pallas_call(
        square_kernel,
        out_shape=(
            jax.ShapeDtypeStruct(other.shape, jnp.float32),
            jax.ShapeDtypeStruct((devices,) + small.shape, jnp.float32),
        ),
        in_specs=[VMEM] * 3,
        out_specs=(VMEM, VMEM),
        compiler_params=pltpu.CompilerParams(vmem_limit_bytes=VMEM_LIMIT),
    )(small, keep, other)


def scale_kernel(slots, entries, message_ref, *refs):
    part_refs = refs[:2]
    step_ref, second_ref, first_bias_ref, bias_ref, loss_ref = refs[2:]
    part = lax.axis_index("dp") % 2
    devices = message_ref.shape[0]
    heads = KEY_VALUE_HEADS
    total = jnp.sum(message_ref[...], axis=0)
    twice = message_ref[0] + message_ref[slots // 2]
    for d in range(2 * slots, devices, 2 * slots):
        twice = twice + message_ref[d] + message_ref[d + slots // 2]
    lines = first_bias_ref.shape[1] // 128
    row = lines * (heads + 1)
    square = total[row : row + 1, 1 + heads : 2 + heads]
    inverse = 1.0 / jnp.sqrt(square / entries + 1e-06)
    share = part_refs[0].shape[0] - 16
    for k in range(2):
        at = pl.ds(pl.multiple_of((part ^ k) * share, share), share)
        step_ref[at, :] = unpack(part_refs[k]) * inverse

    def normal(piece):
        spread = jnp.sum(jnp.sum(piece * piece, axis=0, keepdims=True), axis=1, keepdims=True)
        return 1.0 / jnp.sqrt(spread / piece.size + 1e-06)

    second = total[: lines * heads]
    second = second * normal(second)
    first_bias = twice[lines * heads : row]
    first_bias = first_bias * normal(first_bias)
    for c in range(lines):
        at = slice(c * 128, (c + 1) * 128)
        second_ref[:, at] = second[c * heads : (c + 1) * heads]
        first_bias_ref[:, at] = first_bias[c : c + 1]
    last = twice[row : row + 1]
    lane = lax.broadcasted_iota(jnp.int32, (1, 128), 1)
    loss_ref[0] = jnp.sum(jnp.where(lane == 0, last, 0.0))
    for head in range(heads):
        bias_ref[head] = jnp.sum(jnp.where(lane == 1 + head, last, 0.0))


def scaled(message, parts, slots, entries):
    share, units = parts[0].shape[0] - 16, parts[0].shape[1]
    return pl.pallas_call(
        functools.partial(scale_kernel, slots, entries),
        out_shape=(
            jax.ShapeDtypeStruct((2 * share, units), jnp.float32),
            jax.ShapeDtypeStruct((KEY_VALUE_HEADS, units), jnp.float32),
            jax.ShapeDtypeStruct((1, units), jnp.float32),
            jax.ShapeDtypeStruct((KEY_VALUE_HEADS,), jnp.float32),
            jax.ShapeDtypeStruct((1,), jnp.float32),
        ),
        in_specs=[VMEM] * 3,
        out_specs=(VMEM, VMEM, VMEM, SMEM, SMEM),
        compiler_params=pltpu.CompilerParams(vmem_limit_bytes=VMEM_LIMIT),
    )(message, *parts)


def per_device(
    queries,
    rotated_key_rows,
    hidden_states,
    block_order,
    first_weight,
    first_bias,
    output_weight,
    output_bias,
):
    seq, dp = lax.axis_size("seq"), lax.axis_size("dp")
    rows, model = hidden_states.shape[1:]
    units = first_weight.shape[1]
    tokens = hidden_states.reshape(rows, model)

    keys = rotated_key_rows.reshape(rows, -1)
    far = far_keys(keys)
    turned, hidden, falls = prepare(
        tokens, first_weight, first_bias, output_weight, output_bias, seq
    )
    falls, *far = lax.optimization_barrier((falls, *far))
    stacks, arrived = key_stacks(keys, far)
    falls = gather_near(falls.astype(jnp.float16))
    turned, _ = lax.optimization_barrier((turned, arrived[1]))

    side = seq // 2
    groups = [
        [(d + k) * seq + h * side + r for r in range(side) for k in range(2)]
        for d in range(0, dp, 2)
        for h in range(2)
    ]
    columns = lax.all_to_all(
        turned.reshape(seq, -1, rows), ("dp", "seq"), 0, 0, tiled=True, axis_index_groups=groups
    )
    front, *falls = lax.optimization_barrier((queries.reshape(rows, -1), *falls))
    message = attention_mass(block_order, front, stacks, seq)
    falls = jnp.concatenate(falls, axis=0)
    falls = [falls.astype(jnp.float32), swap(falls, "seq", 1).astype(jnp.float32)]
    message = message + swap(message, "seq", 1)
    mask = 2
    while mask < seq // 4:
        other, *falls = lax.optimization_barrier((swap(message, "seq", mask), *falls))
        message = message + other
        mask *= 2
    top = seq // 4
    message = (message[0] + swap(message[0], "seq", top)) + (
        swap(message[1], "seq", 2 * top) + swap(message[1], "seq", 3 * top)
    )
    keep, send, own_mass, small = gradient(
        (message, swap(message, "dp", 1)), columns, output_weight, hidden, falls
    )
    mask = 2
    while mask < dp:
        keep = keep + swap(keep, "dp", mask)
        send = send + swap(send, "dp", mask)
        mask *= 2
    other = swap(halved(send)[1], "seq", side).astype(jnp.float32)
    total, small = squares(small, keep, other, dp * seq)
    sent, total = lax.optimization_barrier((halved(total)[1], total))
    totals = [halved(total)[0], swap(sent, "dp", 1).astype(jnp.float32)]
    message = lax.all_to_all(small, ("dp", "seq"), 0, 0, tiled=True)
    step_first, second, bias_step, bias, loss = scaled(
        message, totals, seq, model * units * (dp // 2)
    )
    return (
        own_mass.reshape(1, KEY_VALUE_HEADS, rows),
        loss.reshape(()),
        step_first,
        second,
        bias_step.reshape(units),
        bias,
    )


def solution(mesh):
    tokens = P("dp", "seq", None)
    return jax.shard_map(
        per_device,
        mesh=mesh,
        in_specs=(tokens, tokens, tokens, P(), P(), P(), P(), P()),
        out_specs=(P("dp", None, "seq"), P(), P("seq", None), P(), P(), P()),
        check_vma=False,
    )
```

```python
import functools

import jax
import jax.numpy as jnp
from jax import lax
from jax.experimental import pallas as pl
from jax.experimental.pallas import tpu as pltpu
from jax.sharding import PartitionSpec as P

KEY_VALUE_HEADS = 4
HEAD_SIZE = 128
BLK = 64
QUERY_GROUP_SIZE = 8
LOG2_E = 1.4426950408889634
PREDICTED_SCALE = 1.0 / 16.0
VMEM_LIMIT = 40 * 1024 * 1024
PREPARE_VMEM_LIMIT = 60 * 1024 * 1024
VMEM = pl.BlockSpec(memory_space=pltpu.VMEM)
SMEM = pl.BlockSpec(memory_space=pltpu.SMEM)
ANYWHERE = pl.BlockSpec(memory_space=pl.ANY)


def swap(value, axis, mask):
    return lax.ppermute(value, axis, [(i, i ^ mask) for i in range(lax.axis_size(axis))])


def far_groups(amount):
    top = amount // 4
    return [[0], [top], [2 * top, 3 * top]]


def key_masks(amount):
    masks = []
    for near in range(0, amount // 4, 2):
        for group in far_groups(amount):
            masks += [[mask ^ near for mask in group], [mask ^ near ^ 1 for mask in group]]
    return masks


def far_keys(value):
    top = lax.axis_size("seq") // 4
    return [swap(value, "seq", step * top) for step in (1, 2, 3)]


def key_stacks(value, far):
    stacks, arrived = [], []
    for near in range(0, lax.axis_size("seq") // 4, 2):
        for stack in (value[None], far[0][None], jnp.stack(far[1:])):
            if near:
                stack = swap(stack, "seq", near)
                arrived.append(stack)
            stacks += [stack, swap(stack, "seq", 1)]
    return stacks, arrived


def near_order(amount):
    order = [0]
    mask = 2
    while mask < amount // 4:
        order = order + [at ^ mask for at in order]
        mask *= 2
    return [(d, at ^ far) for d in (0, 1) for far in (0, amount // 4) for at in order]


def gather_near(value):
    dp, seq = lax.axis_size("dp"), lax.axis_size("seq")
    slots = [value]
    mask = 2
    while mask < seq // 4:
        slots = slots + [swap(slot, "seq", mask) for slot in slots]
        mask *= 2
    stacked = jnp.stack(slots)
    gathered = [stacked]
    for d, at in ((0, seq // 4), (1, 0), (1, seq // 4)):
        pairs = [(i * seq + j, (i ^ d) * seq + (j ^ at)) for i in range(dp) for j in range(seq)]
        gathered.append(lax.ppermute(stacked, ("dp", "seq"), pairs))
    return gathered


def pack(ref, value):
    rows = value.shape[0]
    reach = jnp.max(jnp.max(jnp.abs(value), axis=0, keepdims=True), axis=1, keepdims=True)
    power = jnp.ceil(jnp.log2(jnp.maximum(reach, 1e-30)))
    ref[:rows, :] = value * jnp.exp2(-power)
    ref[rows:, :] = jnp.broadcast_to(power, (ref.shape[0] - rows, value.shape[1]))


def unpack(ref):
    rows = ref.shape[0] - 16
    return ref[:rows, :] * jnp.exp2(ref[rows : rows + 1, :])


def halved(value):
    value = lax.reduce_precision(value, exponent_bits=5, mantissa_bits=10)
    return value, value.astype(jnp.float16)


def split3(value):
    high = value.astype(jnp.bfloat16)
    rest = value - high.astype(jnp.float32)
    middle = rest.astype(jnp.bfloat16)
    low = (rest - middle.astype(jnp.float32)).astype(jnp.bfloat16)
    return high, middle, low


def prepare_kernel(
    chunks,
    tokens_ref,
    weight_ref,
    bias_ref,
    output_ref,
    output_bias_ref,
    turned_ref,
    hidden_ref,
    fall_ref,
    tokens,
    weight,
    turned,
    copied,
):
    rows = tokens.shape[1]
    block = tokens.shape[2]
    held = turned.shape[1]
    half = chunks // 2

    def copy_in(c):
        at = pl.ds(c * block, block)
        return (
            pltpu.make_async_copy(tokens_ref.at[:, at], tokens.at[c], copied.at[0, c]),
            pltpu.make_async_copy(weight_ref.at[at], weight.at[c], copied.at[1, c]),
        )

    def copy_out(c):
        at = turned_ref.at[pl.ds(c % half * held, held), c // half]
        return pltpu.make_async_copy(turned.at[c], at, copied.at[2, c])

    for c in range(chunks):
        for copy in copy_in(c):
            copy.start()
    pre_act = jnp.broadcast_to(bias_ref[...], hidden_ref.shape)
    for c in range(chunks):
        for copy in copy_in(c):
            copy.wait()
        part = tokens[c]
        turned[c] = jnp.transpose(part).reshape(turned.shape[1:])
        copy_out(c).start()
        pre_act = pre_act + jnp.dot(part, weight[c], preferred_element_type=jnp.float32)
    gate = jax.nn.sigmoid(pre_act)
    hidden = (pre_act * gate).astype(jnp.bfloat16)
    hidden_ref[...] = hidden
    predicted = lax.dot_general(
        output_ref[...], hidden, (((1,), (1,)), ((), ())), preferred_element_type=jnp.float32
    )
    heads = predicted.shape[0]
    head = lax.broadcasted_iota(jnp.int32, predicted.shape, 0)
    for k in range(heads):
        predicted = predicted + jnp.where(head == k, output_bias_ref[k], 0.0)
    fall = gate * (1.0 + pre_act * (1.0 - gate))
    reach = jnp.maximum(jnp.max(jnp.abs(fall), axis=1, keepdims=True), 1e-30)
    power = jnp.ceil(jnp.log2(reach))
    fall_ref[:rows, :] = fall * jnp.exp2(-power)
    fall_ref[rows:, :] = jnp.zeros((fall_ref.shape[0] - rows, fall.shape[1]), jnp.float32)
    for k, piece in enumerate(split3(predicted * PREDICTED_SCALE)):
        fall_ref[rows + k * heads : rows + (k + 1) * heads, :rows] = piece.astype(jnp.float32)
    power = jnp.transpose(jnp.broadcast_to(power, (rows, rows)))[:1]
    fall_ref[rows + 3 * heads : rows + 3 * heads + 1, :rows] = power
    for c in range(chunks):
        copy_out(c).wait()


def prepare(tokens, first_weight, first_bias, output_weight, output_bias, slots):
    rows, model = tokens.shape
    units = first_weight.shape[1]
    share = model // slots // 2
    block = max(share, min(1024, model // 2))
    chunks = model // block
    anywhere = pl.BlockSpec(memory_space=pl.ANY)
    return pl.pallas_call(
        functools.partial(prepare_kernel, chunks),
        out_shape=(
            jax.ShapeDtypeStruct((slots, 2, share, rows), jnp.bfloat16),
            jax.ShapeDtypeStruct((rows, units), jnp.bfloat16),
            jax.ShapeDtypeStruct((rows + 16, units), jnp.float32),
        ),
        in_specs=[anywhere, anywhere, VMEM, VMEM, SMEM],
        out_specs=(anywhere, VMEM, VMEM),
        scratch_shapes=[
            pltpu.VMEM((chunks, rows, block), jnp.bfloat16),
            pltpu.VMEM((chunks, block, units), jnp.bfloat16),
            pltpu.VMEM((chunks, block // share, share, rows), jnp.bfloat16),
            pltpu.SemaphoreType.DMA((3, chunks)),
        ],
        compiler_params=pltpu.CompilerParams(vmem_limit_bytes=PREPARE_VMEM_LIMIT),
        cost_estimate=pl.CostEstimate(
            flops=2 * rows * model * units,
            bytes_accessed=2 * model * (units + 2 * rows),
            transcendentals=rows * units,
        ),
    )(tokens, first_weight, first_bias[None], output_weight, output_bias)


def attention_kernel(slots, order_ref, query_ref, *refs):
    masks = key_masks(slots)
    key_refs, mass_ref = refs[: len(masks)], refs[len(masks)]
    keys, bias, scores, shares = refs[len(masks) + 1 :]
    rows = query_ref.shape[0]
    from_slot = {mask: (i, j) for i, group in enumerate(masks) for j, mask in enumerate(group)}
    total = rows * slots
    lanes = scores.shape[2]
    fold = lanes // rows
    blocks = rows // BLK
    me = lax.axis_index("seq")
    scale = HEAD_SIZE ** (-0.5) * LOG2_E

    def pos_of(owner, index):
        at = jnp.zeros(index.shape, jnp.int32)
        for b in range(blocks):
            at = jnp.where(index // BLK == b, order_ref[owner * blocks + b], at)
        return at * BLK + index % BLK

    side = slots // 2
    query_pos = pos_of(me, lax.broadcasted_iota(jnp.int32, (rows, rows), 1))
    key_index = lax.broadcasted_iota(jnp.int32, (rows, rows), 0)
    for k in range(slots):
        at = pl.ds(k * rows, rows)
        for head in range(KEY_VALUE_HEADS):
            i, j = from_slot[k]
            keys[head, at, :] = key_refs[i][j, :, head * HEAD_SIZE : (head + 1) * HEAD_SIZE]
        bias[at, :] = jnp.where(pos_of(me ^ k, key_index) <= query_pos, 0.0, -1e30)

    def visit_head(head, carried):
        def visit_pair(pair):
            start = head * QUERY_GROUP_SIZE + pair * fold
            query = jnp.concatenate(
                [
                    query_ref[:, pl.ds(pl.multiple_of((start + j) * HEAD_SIZE, HEAD_SIZE), HEAD_SIZE)]
                    for j in range(fold)
                ],
                axis=0,
            )
            query = jnp.transpose(query)
            tops, sums = [], []
            for k in range(slots):
                at = pl.ds(k * rows, rows)
                raw = lax.dot_general(
                    keys[head, at, :],
                    query,
                    (((1,), (0,)), ((), ())),
                    preferred_element_type=jnp.float32,
                )
                raw = (raw + jnp.concatenate([bias[at, :]] * fold, axis=1)).reshape(-1, 8, lanes)
                top = jnp.max(raw, axis=0)
                weight = jnp.exp2((raw - top[None]) * scale)
                scores[pair, at, :] = weight.reshape(rows, lanes)
                tops.append(top)
                sums.append(jnp.sum(weight, axis=0))
            best = functools.reduce(jnp.maximum, tops)
            best = jnp.max(best, axis=0, keepdims=True)
            parts = [jnp.exp2((top - best) * scale) for top in tops]
            summed = sum(part * one for part, one in zip(parts, sums))
            share = (1.0 / QUERY_GROUP_SIZE) / jnp.sum(summed, axis=0, keepdims=True)
            for k in range(slots):
                shares[pair, k] = parts[k] * share

        for pair in range(QUERY_GROUP_SIZE // fold):
            visit_pair(pair)
        for k in range(slots):
            tile = jnp.zeros((rows // 8, 8, rows), jnp.float32)
            for pair in range(QUERY_GROUP_SIZE // fold):
                part = scores[pair, pl.ds(k * rows, rows), :].reshape(rows // 8, 8, lanes)
                part = part * shares[pair, k][None]
                for j in range(fold):
                    tile = tile + part[:, :, j * rows : (j + 1) * rows]
            tile = jnp.transpose(tile.reshape(rows, rows))
            row = jnp.sum(tile, axis=0, keepdims=True)
            mass_ref[k // side, (me ^ k) % side, pl.ds(head, 1), :] = row
        return carried

    lax.fori_loop(0, KEY_VALUE_HEADS, visit_head, 0)


def attention_mass(block_order, queries, stacks, slots):
    rows = queries.shape[0]
    total = rows * slots
    lanes = 2 * rows
    work = total * rows * KEY_VALUE_HEADS * QUERY_GROUP_SIZE
    shape = (2, slots // 2, KEY_VALUE_HEADS, rows)
    return pl.pallas_call(
        functools.partial(attention_kernel, slots),
        out_shape=jax.ShapeDtypeStruct(shape, jnp.float32),
        in_specs=[SMEM] + [VMEM] * (len(stacks) + 1),
        out_specs=VMEM,
        scratch_shapes=[
            pltpu.VMEM((KEY_VALUE_HEADS, total, HEAD_SIZE), jnp.bfloat16),
            pltpu.VMEM((total, rows), jnp.float32),
            pltpu.VMEM((QUERY_GROUP_SIZE * rows // lanes, total, lanes), jnp.float32),
            pltpu.VMEM((QUERY_GROUP_SIZE * rows // lanes, slots, 8, lanes), jnp.float32),
        ],
        compiler_params=pltpu.CompilerParams(vmem_limit_bytes=VMEM_LIMIT),
        cost_estimate=pl.CostEstimate(
            flops=100 * work * HEAD_SIZE, bytes_accessed=2 * queries.size, transcendentals=work
        ),
    )(block_order, queries, *stacks)


def gradient_kernel(slots, columns_ref, output_ref, hidden_ref, *refs):
    message_refs, fall_refs = refs[:2], refs[2:4]
    keep_ref, send_ref, mass_ref, small_ref = refs[4:8]
    slope, wide, grad, columns, copied = refs[8:]
    copy = pltpu.make_async_copy(columns_ref, columns, copied)
    copy.start()
    me, part = lax.axis_index("seq"), lax.axis_index("dp") % 2
    rows = hidden_ref.shape[0]
    total = rows * slots
    units = hidden_ref.shape[1]
    heads = KEY_VALUE_HEADS
    side = slots // 2
    mass_ref[...] = message_refs[0][me % side]
    output_rows = output_ref[...]
    output_three = jnp.concatenate([output_rows] * 3, axis=0)
    first_bias = jnp.zeros((8, units), jnp.float32)
    squared = jnp.zeros((heads, rows), jnp.float32)
    grad_bias = jnp.zeros((heads, rows), jnp.float32)
    order = near_order(slots)
    for j in range(slots):
        d, mask = order[j // 2]
        mask = mask + j % 2
        held = fall_refs[j % 2][j // 2]
        beside = held[rows:, :rows]
        predicted = (beside[:heads] + beside[heads : 2 * heads]) + beside[2 * heads : 3 * heads]
        mass = message_refs[d][(me ^ mask) % side]
        residue = predicted * (1.0 / PREDICTED_SCALE) - jnp.log(1.0 + mass)
        out_grad = residue / total
        if j == 0:
            own_grad = out_grad
        squared = squared + residue * residue
        grad_bias = grad_bias + out_grad
        scaled = out_grad * jnp.exp2(beside[3 * heads : 3 * heads + 1])
        back = lax.dot_general(
            jnp.concatenate(split3(scaled), axis=0),
            output_three,
            (((0,), (0,)), ((), ())),
            preferred_element_type=jnp.float32,
        )
        fall = back * held[:rows]
        first_bias = first_bias + jnp.sum(fall.reshape(rows // 8, 8, units), axis=0)
        at = slice(j * rows, (j + 1) * rows)
        slope[at, :] = fall.astype(jnp.bfloat16)
    loss_sum = jnp.sum(squared) * (0.5 / total)
    grad_bias = jnp.sum(grad_bias, axis=1, keepdims=True)
    copy.wait()
    for j in range(slots):
        d, mask = order[j // 2]
        mask = mask + j % 2
        at = slice(j * rows, (j + 1) * rows)
        wide[:, at] = columns[2 * ((me ^ mask) % side) + (part ^ d)]
    grad[...] = jnp.dot(wide[...], slope[...], preferred_element_type=jnp.float32)
    share = keep_ref.shape[0]
    low = pl.multiple_of((me // side) * share, share)
    keep_ref[...] = grad[pl.ds(low, share), :]
    pack(send_ref, grad[pl.ds(pl.multiple_of(share - low, share), share), :])
    second = lax.dot_general(
        jnp.concatenate(split3(own_grad), axis=0),
        hidden_ref[...],
        (((1,), (0,)), ((), ())),
        preferred_element_type=jnp.float32,
    )
    second = second[:heads] + second[heads : 2 * heads] + second[2 * heads :]
    lines = units // 128
    first_bias = jnp.sum(first_bias, axis=0, keepdims=True)
    small_ref[...] = jnp.zeros_like(small_ref)
    for c in range(lines):
        at = slice(c * 128, (c + 1) * 128)
        small_ref[pl.ds(c * heads, heads), :] = second[:, at]
        small_ref[pl.ds(lines * heads + c, 1), :] = first_bias[:, at]
    lane = lax.broadcasted_iota(jnp.int32, (1, 128), 1)
    last = jnp.where(lane == 0, loss_sum, 0.0)
    for head in range(heads):
        last = jnp.where(lane == 1 + head, grad_bias[head : head + 1], last)
    small_ref[pl.ds(lines * (heads + 1), 1), :] = last


def gradient(messages, columns, output_weight, hidden, falls):
    slots, depth, rows = columns.shape
    units = hidden.shape[1]
    return pl.pallas_call(
        functools.partial(gradient_kernel, slots),
        out_shape=(
            jax.ShapeDtypeStruct((depth // 2, units), jnp.float32),
            jax.ShapeDtypeStruct((depth // 2 + 16, units), jnp.float32),
            jax.ShapeDtypeStruct((KEY_VALUE_HEADS, rows), jnp.float32),
            jax.ShapeDtypeStruct((small_rows(units), 128), jnp.float32),
        ),
        in_specs=[ANYWHERE] + [VMEM] * 6,
        out_specs=(VMEM,) * 4,
        scratch_shapes=[
            pltpu.VMEM((slots * rows, units), jnp.bfloat16),
            pltpu.VMEM((depth, slots * rows), jnp.bfloat16),
            pltpu.VMEM((depth, units), jnp.float32),
            pltpu.VMEM(columns.shape, jnp.bfloat16),
            pltpu.SemaphoreType.DMA,
        ],
        compiler_params=pltpu.CompilerParams(vmem_limit_bytes=VMEM_LIMIT),
        cost_estimate=pl.CostEstimate(
            flops=2 * depth * slots * rows * units,
            bytes_accessed=2 * columns.size + 8 * slots * rows * units,
            transcendentals=0,
        ),
    )(columns, output_weight, hidden, *messages, *falls)


def small_rows(units):
    return -(-(units // 128 * (KEY_VALUE_HEADS + 1) + 1) // 8) * 8


def square_kernel(small_ref, keep_ref, other_ref, total_ref, send_ref):
    total = keep_ref[...] + unpack(other_ref)
    pack(total_ref, total)
    square = jnp.sum(jnp.sum(total * total, axis=0, keepdims=True), axis=1, keepdims=True)
    row = total.shape[1] // 128 * (KEY_VALUE_HEADS + 1)
    lane = lax.broadcasted_iota(jnp.int32, (1, 128), 1)
    last = jnp.where(lane == 1 + KEY_VALUE_HEADS, square, small_ref[row : row + 1, :])
    for k in range(send_ref.shape[0]):
        send_ref[k] = small_ref[...]
        send_ref[k, row : row + 1, :] = last


def squares(small, keep, other, devices):
    return pl.pallas_call(
        square_kernel,
        out_shape=(
            jax.ShapeDtypeStruct(other.shape, jnp.float32),
            jax.ShapeDtypeStruct((devices,) + small.shape, jnp.float32),
        ),
        in_specs=[VMEM] * 3,
        out_specs=(VMEM, VMEM),
        compiler_params=pltpu.CompilerParams(vmem_limit_bytes=VMEM_LIMIT),
    )(small, keep, other)


def scale_kernel(slots, entries, message_ref, *refs):
    part_refs = refs[:2]
    step_ref, second_ref, first_bias_ref, bias_ref, loss_ref = refs[2:]
    part = lax.axis_index("dp") % 2
    devices = message_ref.shape[0]
    heads = KEY_VALUE_HEADS
    total = jnp.sum(message_ref[...], axis=0)
    twice = message_ref[0] + message_ref[slots // 2]
    for d in range(2 * slots, devices, 2 * slots):
        twice = twice + message_ref[d] + message_ref[d + slots // 2]
    lines = first_bias_ref.shape[1] // 128
    row = lines * (heads + 1)
    square = total[row : row + 1, 1 + heads : 2 + heads]
    inverse = 1.0 / jnp.sqrt(square / entries + 1e-06)
    share = part_refs[0].shape[0] - 16
    for k in range(2):
        at = pl.ds(pl.multiple_of((part ^ k) * share, share), share)
        step_ref[at, :] = unpack(part_refs[k]) * inverse

    def normal(piece):
        spread = jnp.sum(jnp.sum(piece * piece, axis=0, keepdims=True), axis=1, keepdims=True)
        return 1.0 / jnp.sqrt(spread / piece.size + 1e-06)

    second = total[: lines * heads]
    second = second * normal(second)
    first_bias = twice[lines * heads : row]
    first_bias = first_bias * normal(first_bias)
    for c in range(lines):
        at = slice(c * 128, (c + 1) * 128)
        second_ref[:, at] = second[c * heads : (c + 1) * heads]
        first_bias_ref[:, at] = first_bias[c : c + 1]
    last = twice[row : row + 1]
    lane = lax.broadcasted_iota(jnp.int32, (1, 128), 1)
    loss_ref[0] = jnp.sum(jnp.where(lane == 0, last, 0.0))
    for head in range(heads):
        bias_ref[head] = jnp.sum(jnp.where(lane == 1 + head, last, 0.0))


def scaled(message, parts, slots, entries):
    share, units = parts[0].shape[0] - 16, parts[0].shape[1]
    return pl.pallas_call(
        functools.partial(scale_kernel, slots, entries),
        out_shape=(
            jax.ShapeDtypeStruct((2 * share, units), jnp.float32),
            jax.ShapeDtypeStruct((KEY_VALUE_HEADS, units), jnp.float32),
            jax.ShapeDtypeStruct((1, units), jnp.float32),
            jax.ShapeDtypeStruct((KEY_VALUE_HEADS,), jnp.float32),
            jax.ShapeDtypeStruct((1,), jnp.float32),
        ),
        in_specs=[VMEM] * 3,
        out_specs=(VMEM, VMEM, VMEM, SMEM, SMEM),
        compiler_params=pltpu.CompilerParams(vmem_limit_bytes=VMEM_LIMIT),
    )(message, *parts)


def per_device(
    queries,
    rotated_key_rows,
    hidden_states,
    block_order,
    first_weight,
    first_bias,
    output_weight,
    output_bias,
):
    seq, dp = lax.axis_size("seq"), lax.axis_size("dp")
    rows, model = hidden_states.shape[1:]
    units = first_weight.shape[1]
    tokens = hidden_states.reshape(rows, model)

    keys = rotated_key_rows.reshape(rows, -1)
    far = far_keys(keys)
    turned, hidden, falls = prepare(
        tokens, first_weight, first_bias, output_weight, output_bias, seq
    )
    falls, *far = lax.optimization_barrier((falls, *far))
    stacks, arrived = key_stacks(keys, far)
    falls = gather_near(falls.astype(jnp.float16))
    turned, _ = lax.optimization_barrier((turned, arrived[1]))

    side = seq // 2
    groups = [
        [(d + k) * seq + h * side + r for r in range(side) for k in range(2)]
        for d in range(0, dp, 2)
        for h in range(2)
    ]
    columns = lax.all_to_all(
        turned.reshape(seq, -1, rows), ("dp", "seq"), 0, 0, tiled=True, axis_index_groups=groups
    )
    front, *falls = lax.optimization_barrier((queries.reshape(rows, -1), *falls))
    message = attention_mass(block_order, front, stacks, seq)
    falls = jnp.concatenate(falls, axis=0)
    falls = [falls.astype(jnp.float32), swap(falls, "seq", 1).astype(jnp.float32)]
    message = message + swap(message, "seq", 1)
    mask = 2
    while mask < seq // 4:
        other, *falls = lax.optimization_barrier((swap(message, "seq", mask), *falls))
        message = message + other
        mask *= 2
    top = seq // 4
    message = (message[0] + swap(message[0], "seq", top)) + (
        swap(message[1], "seq", 2 * top) + swap(message[1], "seq", 3 * top)
    )
    keep, send, own_mass, small = gradient(
        (message, swap(message, "dp", 1)), columns, output_weight, hidden, falls
    )
    mask = 2
    while mask < dp:
        keep = keep + swap(keep, "dp", mask)
        send = send + swap(send, "dp", mask)
        mask *= 2
    other = swap(halved(send)[1], "seq", side).astype(jnp.float32)
    total, small = squares(small, keep, other, dp * seq)
    sent, total = lax.optimization_barrier((halved(total)[1], total))
    totals = [halved(total)[0], swap(sent, "dp", 1).astype(jnp.float32)]
    message = lax.all_to_all(small, ("dp", "seq"), 0, 0, tiled=True)
    step_first, second, bias_step, bias, loss = scaled(
        message, totals, seq, model * units * (dp // 2)
    )
    return (
        own_mass.reshape(1, KEY_VALUE_HEADS, rows),
        loss.reshape(()),
        step_first,
        second,
        bias_step.reshape(units),
        bias,
    )


def solution(mesh):
    tokens = P("dp", "seq", None)
    return jax.shard_map(
        per_device,
        mesh=mesh,
        in_specs=(tokens, tokens, tokens, P(), P(), P(), P(), P()),
        out_specs=(P("dp", None, "seq"), P(), P("seq", None), P(), P(), P()),
        check_vma=False,
    )
```
